256 devices in a mesh: table: 64 (over y, z, core), col: 4 (over x).
Axes of the slice: x: 4, y: 4, z: 8, core: 2. Of those that a mesh axis runs over, the one named last changes fastest.
Arguments:
- embedding: bfloat16 [262144, 256], P('table', 'col'), may hold values from -4 to 4
- accumulator: float32 [262144, 256], P('table', 'col'), may hold values from 0.01 to 1
- pair_rows: int32 [16384, 128, 4], P(('table', 'col')), may hold values from 0 to 1023
- pair_len: int32 [16384, 128], P(('table', 'col')), may hold values from 0 to 4
- pair_dest: int32 [256, 64], P(('table', 'col')), may hold values from 0 to 63, each once within a row
- pair_tile: int32 [256, 64], P(('table', 'col')), may hold values from 0 to 15
- pooled_grad: bfloat16 [524288, 256], P(('table', 'col')), may hold values from -6 to 6
Outputs:
- pooled: bfloat16 [524288, 256], P(('table', 'col'))
- new_embedding: bfloat16 [262144, 256], P(('table', 'col'))
- new_accumulator: float32 [262144, 256], P(('table', 'col'))
The draws below stay inside these ranges and needn't reach their ends.
Inputs may be any that keep to these rules, and one draw needn't show every extreme that they name: `pair_dest`: each row names every table index exactly once.
All inputs are finite; a program needn't handle non-finite values.
Results may differ from the reference program's by a relative error of at most 0.0049.
Values may be sent and summed in bfloat16 or wider, within the bound.
A program may use at most 128 MiB of HBM per device.

```python
import math
import jax
import jax.numpy as jnp
from jax import lax

DIM = 256
BLOCK = 128
LOOK = 4
R_DEV = 1024
TILE_DEV = 16
PAIRS = 64
ROWS = 262144
BAGS = 524288
N_TABLE = 64
N_COL = 4
DEVICES = 256


def touch_ends(drawn, stream_key, smallest, high):
    longest = drawn.shape.index(max(drawn.shape))
    spots = []
    for shift in (0, 1):
        where = [jax.random.randint(jax.random.fold_in(stream_key, axis), (), 0, length) for axis, length in enumerate(drawn.shape)]
        where[longest] = (where[longest] + shift) % drawn.shape[longest]
        spots.append(tuple(where))
    return drawn.at[spots[0]].set(smallest).at[spots[1]].set(high)


def block_scale(stream_key, extent, shards, smallest, top_value):
    loudness, own = 1.0, jax.random.fold_in(stream_key, 6)
    for dim, shards_of in shards:
        draws = jnp.exp(jax.random.uniform(jax.random.fold_in(own, dim), (shards_of,), jnp.float32, smallest / len(shards), top_value / len(shards)))
        loudness = loudness * jnp.repeat(draws, extent[dim] // shards_of).reshape([-1 if axis == dim else 1 for axis in range(len(extent))])
    return loudness


def centred(own_key, extent, deviation, reach, pieces=(), held_as=jnp.bfloat16):
    entries = deviation * jax.random.normal(own_key, extent, jnp.float32)
    if pieces:
        entries = entries * block_scale(own_key, extent, pieces, -0.22, 0.18)
    return jnp.clip(entries, -reach, reach).astype(held_as)


def setup_inputs(seed: int = 0) -> dict:
    key_of = jax.random.split(jax.random.key(seed), 8)
    return {
        "embedding": centred(key_of[0], (ROWS, DIM), 0.5, 4.0, ((0, 64), (1, 4))),
        "accumulator": jnp.clip(jnp.exp(math.log(1.0) - 4.6051702 * jax.random.uniform(key_of[1], (ROWS, DIM), jnp.float32) ** block_scale(key_of[1], (ROWS, DIM), ((0, 64), (1, 4)), -0.2, 0.2)), 0.01, 1.0),
        "pair_rows": touch_ends(jax.random.randint(key_of[2], (DEVICES * PAIRS, BLOCK, LOOK), 0, R_DEV), jax.random.fold_in(key_of[2], 1), 0, R_DEV - 1).astype(jnp.int32),
        "pair_len": touch_ends(jax.random.randint(key_of[3], (DEVICES * PAIRS, BLOCK), 0, LOOK + 1), jax.random.fold_in(key_of[3], 1), 0, LOOK).astype(jnp.int32),
        "pair_dest": jax.vmap(lambda own: jax.random.permutation(own, N_TABLE))(jax.random.split(key_of[4], DEVICES)).reshape((DEVICES, PAIRS)).astype(jnp.int32),
        "pair_tile": touch_ends(jax.random.randint(key_of[5], (DEVICES, PAIRS), 0, TILE_DEV), jax.random.fold_in(key_of[5], 1), 0, TILE_DEV - 1).astype(jnp.int32),
        "pooled_grad": centred(key_of[6], (BAGS, DIM), 1.0, 6.0, ((0, 256),)),
    }


def reference(embedding, accumulator, pair_rows, pair_len, pair_dest, pair_tile, pooled_grad):
    device_count = N_TABLE * N_COL
    rows_all = pair_rows.reshape(device_count, PAIRS, BLOCK, LOOK)
    lens_all = pair_len.reshape(device_count, PAIRS, BLOCK)
    emb_all = embedding.reshape(device_count, R_DEV, DIM)
    acc_all = accumulator.reshape(device_count, R_DEV, DIM)
    grad_tiles = pooled_grad.reshape(device_count * TILE_DEV, BLOCK, DIM)
    owner_ids = jnp.arange(device_count, dtype=jnp.int32)

    def per_owner(total, item):
        owner, emb_rows, acc_rows, rows, lens, dests, tiles = item
        valid = (jnp.arange(LOOK, dtype=jnp.int32)[None, None, :] < lens[:, :, None]).astype(jnp.float32)
        picked = emb_rows[rows].astype(jnp.float32) * valid[..., None]
        partial_value = lax.optimization_barrier(jnp.sum(picked, axis=2)).astype(jnp.bfloat16)
        global_tile = ((dests * N_COL + owner % N_COL) * TILE_DEV + tiles).astype(jnp.int32)
        total = total.at[global_tile].add(partial_value.astype(jnp.float32))
        cot = grad_tiles[global_tile].astype(jnp.float32)
        contrib = cot[:, :, None, :] * valid[..., None]
        grad = jnp.zeros((R_DEV, DIM), jnp.float32).at[rows.reshape(-1)].add(contrib.reshape(-1, DIM))
        new_acc = acc_rows + grad * grad
        new_emb = (emb_rows.astype(jnp.float32) - 0.3 * grad / (jnp.sqrt(new_acc) + 1e-08)).astype(jnp.bfloat16)
        return (total, (new_emb, new_acc))
    start = jnp.zeros((device_count * TILE_DEV, BLOCK, DIM), jnp.float32)
    total, outs = lax.scan(per_owner, start, (owner_ids, emb_all, acc_all, rows_all, lens_all, pair_dest, pair_tile))
    pooled = total.reshape(BAGS, DIM).astype(jnp.bfloat16)
    return (pooled, outs[0].reshape(ROWS, DIM), outs[1].reshape(ROWS, DIM))
```

```python
import functools
import jax
import jax.numpy as jnp
from jax import lax
from jax.experimental import pallas as pl
from jax.experimental.pallas import tpu as pltpu
from jax.sharding import PartitionSpec as P

LEARN_RATE = 0.3
EPSILON = 1e-08
MESH = pl.DeviceIdType.MESH
NY, NZ, NCORE, NX = 4, 8, 2, 4
PLANE = NY * NCORE
ROWS = 1024
DIM = 256
BAGS = 128
LOOK = 4
TILES = 16
FEAT = DIM // NX
SPAN = PLANE * BAGS
TILE_UNIT = 2048
HALF = DIM // 2


def prep_kernel(dest_ref, tile_ref, rows_ref, len_ref, msg_ref):
    look = lax.broadcasted_iota(jnp.int32, (LOOK, BAGS), 0)

    def one(pair, carry):
        dest = dest_ref[0, pair]
        place = (dest // NCORE) % NZ * PLANE + dest // (NCORE * NZ) * NCORE + dest % NCORE
        valid = look < len_ref[pl.ds(pair, 1), :]
        msg_ref[place] = jnp.where(valid, rows_ref[pair], ROWS) + tile_ref[0, pair] * TILE_UNIT
        return carry

    lax.fori_loop(0, NZ * PLANE, one, 0)


def move_kernel(
    emb_ref, acc_ref, msg_ref, cot_ref,
    arr_ref, tiles_ref, grad_ref, own_ref, state_ref,
    emb_all, counts, cot_all, part, tile_rows, idx, gsend, grecv, gsum, chosen, acc_half, acc_own, row_ids, tile_nums,
    ex_s, ex_r, ax_s, ax_r, ix_s, ix_r, e_s, e_r, cy_s, cy_r, cx_s, cx_r, p_s, p_r, t_s, t_r, g_s, g_r, loc,
):
    t = lax.axis_index("table")
    x = lax.axis_index("col")
    y, z, core = t // (NZ * NCORE), (t // NCORE) % NZ, t % NCORE

    def at(yy, zz, cc):
        return (lax.rem(yy + NY, NY) * NZ + lax.rem(zz + NZ, NZ)) * NCORE + lax.rem(cc + NCORE, NCORE)

    def plane(zz):
        return lax.rem(zz + 2 * NZ, NZ)

    def spot(yy, cc):
        return lax.rem(yy + NY, NY) * NCORE + lax.rem(cc + NCORE, NCORE)

    me = spot(y, core)
    others = [(dy, dc) for dy in (2, 1, 3, 0) for dc in (0, 1) if (dy, dc) != (0, 0)]

    barrier = pltpu.get_barrier_semaphore()
    for j in range(1, NX):
        pl.semaphore_signal(barrier, inc=1, device_id=(t, lax.rem(x + j, NX)), device_id_type=MESH)
    for j in range(1, NZ):
        pl.semaphore_signal(barrier, inc=1, device_id=(at(y, z + j, core), x), device_id_type=MESH)
    for dy, dc in others:
        pl.semaphore_signal(barrier, inc=1, device_id=(at(y + dy, z, core + dc), x), device_id_type=MESH)
    pl.semaphore_wait(barrier, NX - 1 + NZ - 1 + PLANE - 1)

    sent = []

    def send(src, dst, send_sem, recv_sem, table, col):
        copy = pltpu.make_async_remote_copy(
            src_ref=src, dst_ref=dst, send_sem=send_sem, recv_sem=recv_sem, device_id=(table, col), device_id_type=MESH
        )
        copy.start()
        sent.append(copy)

    def arrived(dst, recv_sem):
        pltpu.make_async_copy(dst, dst, recv_sem).wait()

    def feature_rows(q):
        return pl.ds(pl.multiple_of(q * FEAT, FEAT), FEAT)

    def lanes(start, size):
        return pl.ds(pl.multiple_of(start, 128), size)

    for j in range(1, NX):
        owner = lax.rem(x + j, NX)
        send(
            emb_ref.at[:, lanes(owner * ROWS, ROWS)], emb_all.at[z, feature_rows(x)],
            ex_s.at[j - 1], ex_r.at[j - 1], t, owner,
        )
    emb_all[z, feature_rows(x), :] = emb_ref[:, lanes(x * ROWS, ROWS)]

    def pass_rows(way, step, order, q):
        source = plane(z - step) if way == 0 else plane(z + step)
        target = plane(z + 1) if way == 0 else plane(z - 1)
        block = emb_all.at[source, feature_rows(q)]
        send(block, block, e_s.at[way, step, order], e_r.at[way, step + 1, order], at(y, target, core), x)

    def wait_rows(way, step, order, q):
        source = plane(z - step) if way == 0 else plane(z + step)
        arrived(emb_all.at[source, feature_rows(q)], e_r.at[way, step, order])

    for way in (0, 1):
        pass_rows(way, 0, 0, x)

    for off in (1, 7, 2, 6, 3, 5, 4):
        target = plane(z + off)
        send(msg_ref.at[target], idx.at[z], ix_s.at[off], ix_r.at[off], at(y, target, core), x)

    def tiles4(c):
        return pl.ds(4 * c, 4)

    for c in range(4):
        for way, dy in ((0, 1), (1, -1)):
            c_way = c if way == 0 else (c + 2) % 4
            send(
                cot_ref.at[tiles4(c_way)], cot_all.at[me, tiles4(c_way)],
                cy_s.at[way, 0, c_way], cy_r.at[way, 1, c_way], at(y + dy, z, core), x,
            )
    for c in range(4):
        send(cot_ref.at[tiles4(c)], cot_all.at[me, tiles4(c)], cx_s.at[0, c], cx_r.at[0, c], at(y, z, core + 1), x)
    own_cot = pltpu.make_async_copy(cot_ref, cot_all.at[me], loc.at[0])
    own_cot.start()

    idx[z] = msg_ref[z]
    acc_half[...] = acc_ref[...].astype(jnp.bfloat16)

    ids = lax.broadcasted_iota(jnp.int32, (DIM, BAGS), 0)
    row_ids[...] = ids.astype(jnp.float32).astype(jnp.bfloat16)

    def build(zo):
        def pair(n, carry):
            held = idx[zo, n]
            tile_rows[n, pl.ds(zo, 1), :] = lax.shift_right_logical(held[:1], 11)
            row = held & (TILE_UNIT - 1)
            for block in range(ROWS // DIM):
                near = jnp.clip(row - block * DIM, -1, DIM).astype(jnp.float32).astype(jnp.bfloat16)
                total = None
                for l in range(LOOK):
                    hit = jnp.where(row_ids[...] == near[l : l + 1], 1.0, 0.0).astype(jnp.bfloat16)
                    total = hit if total is None else total + hit
                counts[zo, pl.ds(block * DIM, DIM), lanes(n * BAGS, BAGS)] = total
            return carry

        lax.fori_loop(0, PLANE, pair, 0)

    def pool(zo, order):
        def block(b, carry):
            got = jnp.dot(
                emb_all[zo], counts[zo, :, lanes(b * DIM, DIM)], preferred_element_type=jnp.float32
            ).astype(jnp.bfloat16)
            part[zo, 2 * b] = got[:, :BAGS]
            part[zo, 2 * b + 1] = got[:, BAGS:]
            return carry

        lax.fori_loop(0, SPAN // DIM, block, 0)
        for k, (dy, dc) in enumerate(others):
            dest = spot(y + dy, core + dc)
            send(part.at[zo, dest], arr_ref.at[me, zo], p_s.at[order, k], p_r.at[order, k], at(y + dy, z, core + dc), x)
        pltpu.make_async_copy(part.at[zo, me], arr_ref.at[me, zo], loc.at[1 + order]).start()

    build(z)
    for j in range(1, NX):
        q = lax.rem(x - j + NX, NX)
        arrived(emb_all.at[z, feature_rows(q)], ex_r.at[j - 1])
        for way in (0, 1):
            pass_rows(way, 0, j, q)
    for j in range(1, NX):
        owner = lax.rem(x + j, NX)
        send(
            acc_half.at[:, lanes(owner * ROWS, ROWS)], acc_own.at[feature_rows(x)],
            ax_s.at[j - 1], ax_r.at[j - 1], t, owner,
        )
    acc_own[feature_rows(x), :] = acc_half[:, lanes(x * ROWS, ROWS)]
    pool(z, 0)

    def relay_cot(way, step, c):
        dy = 1 if way == 0 else -1
        source = spot(y - dy * step, core)
        block = cot_all.at[source, tiles4(c)]
        arrived(block, cy_r.at[way, step, c])
        if step == 1 and c // 2 == way:
            send(block, block, cy_s.at[way, 1, c], cy_r.at[way, 2, c], at(y + dy, z, core), x)
        slot = 1 + way if step == 1 else 3
        send(block, block, cx_s.at[slot, c], cx_r.at[slot, c], at(y, z, core + 1), x)

    order = 1
    for step in range(1, NZ // 2 + 1):
        near, far = plane(z - step), plane(z + step)
        sources = ((near, step), (far, NZ - step)) if step < NZ // 2 else ((near, step),)
        for zo, off in sources:
            arrived(idx.at[zo], ix_r.at[off])
            build(zo)
        if step < NZ // 2:
            for k in range(NX):
                for way, zo in ((0, near), (1, far)):
                    if step > 1 or True:
                        q = lax.rem(x - k + NX, NX)
                        wait_rows(way, step, k, q)
                        if step < NZ // 2 - 1 or (k < NX // 2) == (way == 0):
                            pass_rows(way, step, k, q)
            if step == 1:
                for c in (0, 1):
                    relay_cot(0, 1, c)
                    relay_cot(1, 1, 2 + c)
            if step == 2:
                for c in (0, 1):
                    relay_cot(0, 1, 2 + c)
                    relay_cot(1, 1, c)
            if step == 3:
                for c in (0, 1):
                    relay_cot(0, 2, c)
                    relay_cot(1, 2, 2 + c)
        else:
            for k in range(NX):
                q = lax.rem(x - k + NX, NX)
                wait_rows(0 if k < NX // 2 else 1, step, k, q)
        for zo, off in sources:
            pool(zo, order)
            order += 1

    to_scalars = pltpu.make_async_copy(tile_rows, tile_nums, loc.at[9])
    to_scalars.start()
    for k, (dy, dc) in enumerate(others):
        dest = spot(y + dy, core + dc)
        send(tile_rows.at[dest], tiles_ref.at[me], t_s.at[k], t_r.at[k], at(y + dy, z, core + dc), x)
    tiles_ref[me] = tile_rows[me]
    to_scalars.wait()

    own_cot.wait()
    for c in range(4):
        arrived(cot_all.at[spot(y, core + 1), tiles4(c)], cx_r.at[0, c])
        arrived(cot_all.at[spot(y - 1, core + 1), tiles4(c)], cx_r.at[1, c])
        arrived(cot_all.at[spot(y + 1, core + 1), tiles4(c)], cx_r.at[2, c])
        arrived(cot_all.at[spot(y + 2, core + 1), tiles4(c)], cx_r.at[3, c])

    def gradient(zo):
        def pick(n, carry):
            chosen[pl.ds(pl.multiple_of(n * BAGS, BAGS), BAGS), :] = cot_all[n, tile_nums[n, zo, 0]]
            return carry

        lax.fori_loop(0, PLANE, pick, 0)

        def block(b, carry):
            rows = pl.ds(pl.multiple_of(b * DIM, DIM), DIM)
            gsum[rows, :] = jnp.dot(counts[zo, rows, :], chosen[...], preferred_element_type=jnp.float32)
            return carry

        lax.fori_loop(0, ROWS // DIM, block, 0)

    def pass_grad(way, dist, half, add):
        if add:
            arrived(grecv.at[way, dist, half], g_r.at[way, dist, half])

        def block(b, carry):
            rows = pl.ds(pl.multiple_of(b * DIM, DIM), DIM)
            value = gsum[rows, half * HALF : (half + 1) * HALF]
            if add:
                value = value + grecv[way, dist, half, rows, :].astype(jnp.float32)
            gsend[way, dist - 1, half, rows, :] = value.astype(jnp.bfloat16)
            return carry

        lax.fori_loop(0, ROWS // DIM, block, 0)
        target = plane(z + 1) if way == 0 else plane(z - 1)
        send(
            gsend.at[way, dist - 1, half], grecv.at[way, dist - 1, half],
            g_s.at[way, dist - 1, half], g_r.at[way, dist - 1, half], at(y, target, core), x,
        )

    gradient(plane(z + NZ // 2))
    pass_grad(0, NZ // 2, 0, False)
    pass_grad(1, NZ // 2, 1, False)
    for dist in range(NZ // 2 - 1, 0, -1):
        for way in (0, 1):
            gradient(plane(z + dist) if way == 0 else plane(z - dist))
            late = way
            if dist == NZ // 2 - 1:
                pass_grad(way, dist, 1 - late, False)
                pass_grad(way, dist, late, True)
            else:
                pass_grad(way, dist, 0, True)
                pass_grad(way, dist, 1, True)
    gradient(z)

    for j in range(1, NX):
        arrived(acc_own.at[feature_rows(lax.rem(x - j + NX, NX))], ax_r.at[j - 1])

    def turn(b, carry):
        rows = pl.ds(pl.multiple_of(b * 128, 128), 128)
        own_ref[rows, :] = emb_all[z, :, rows].astype(jnp.float32).T.astype(jnp.bfloat16)
        state_ref[rows, :] = acc_own[:, rows].astype(jnp.float32).T.astype(jnp.bfloat16)
        return carry

    lax.fori_loop(0, ROWS // 128, turn, 0)

    for half in (0, 1):
        for way in (0, 1):
            arrived(grecv.at[way, 0, half], g_r.at[way, 0, half])

    def total(b, carry):
        rows = pl.ds(pl.multiple_of(b * DIM, DIM), DIM)
        for half in (0, 1):
            cols = slice(half * HALF, (half + 1) * HALF)
            grad_ref[rows, cols] = (
                gsum[rows, cols]
                + grecv[0, 0, half, rows, :].astype(jnp.float32)
                + grecv[1, 0, half, rows, :].astype(jnp.float32)
            )
        return carry

    lax.fori_loop(0, ROWS // DIM, total, 0)

    order = 0
    for step in range(NZ // 2 + 1):
        for zo in (plane(z - step), plane(z + step)) if 0 < step < NZ // 2 else (plane(z - step),):
            for k, (dy, dc) in enumerate(others):
                arrived(arr_ref.at[spot(y - dy, core - dc), zo], p_r.at[order, k])
            pltpu.make_async_copy(part.at[zo, me], arr_ref.at[me, zo], loc.at[1 + order]).wait()
            order += 1
    for k, (dy, dc) in enumerate(others):
        arrived(tiles_ref.at[spot(y - dy, core - dc)], t_r.at[k])
    for copy in sent:
        copy.wait_send()


def finish_kernel(tiles_ref, arr_ref, grad_ref, own_ref, state_ref, pooled_ref, rows_ref, sums_ref, total):
    step = pl.program_id(0)

    @pl.when(step == 0)
    def _():
        total[...] = jnp.zeros_like(total)

    def add(k, carry):
        tile = tiles_ref[step, k, 0]
        total[tile] = total[tile] + arr_ref[0, k].astype(jnp.float32)
        return carry

    lax.fori_loop(0, NZ, add, 0)
    grad = grad_ref[...]
    new_state = state_ref[...].astype(jnp.float32) + grad * grad
    sums_ref[...] = new_state
    rows_ref[...] = (
        own_ref[...].astype(jnp.float32) - LEARN_RATE * grad / (jnp.sqrt(new_state) + EPSILON)
    ).astype(jnp.bfloat16)

    @pl.when(step == PLANE - 1)
    def _():
        def turn(k, carry):
            pooled_ref[k] = total[k].T.astype(jnp.bfloat16)
            return carry

        lax.fori_loop(0, TILES, turn, 0)


def per_device(embedding, accumulator, pair_rows, pair_len, pair_dest, pair_tile, pooled_grad):
    smem = pl.BlockSpec(memory_space=pltpu.SMEM)
    vmem = pl.BlockSpec(memory_space=pltpu.VMEM)
    hbm = pl.BlockSpec(memory_space=pl.ANY)
    bf16, f32, i32 = jnp.bfloat16, jnp.float32, jnp.int32
    msg = pl.pallas_call(
        prep_kernel,
        out_shape=jax.ShapeDtypeStruct((NZ * PLANE, LOOK, BAGS), i32),
        in_specs=[smem, smem, vmem, vmem],
        out_specs=vmem,
        name="sort_pairs",
    )(pair_dest, pair_tile, jnp.transpose(pair_rows, (0, 2, 1)), pair_len)
    msg = msg.reshape(NZ, PLANE, LOOK, BAGS)
    dma = pltpu.SemaphoreType.DMA
    sems = [(3,), (3,), (3,), (3,), (8,), (8,), (2, 5, 4), (2, 5, 4), (2, 3, 4), (2, 3, 4), (4, 4), (4, 4),
            (8, 7), (8, 7), (7,), (7,), (2, 4, 2), (2, 4, 2), (10,)]
    arr, tiles, grad, own, state = pl.pallas_call(
        move_kernel,
        out_shape=(
            jax.ShapeDtypeStruct((PLANE, NZ, DIM, BAGS), bf16),
            jax.ShapeDtypeStruct((PLANE, NZ, BAGS), i32),
            jax.ShapeDtypeStruct((ROWS, DIM), f32),
            jax.ShapeDtypeStruct((ROWS, DIM), bf16),
            jax.ShapeDtypeStruct((ROWS, DIM), bf16),
        ),
        in_specs=[vmem, vmem, vmem, hbm],
        out_specs=(hbm, vmem, vmem, vmem, vmem),
        scratch_shapes=[
            pltpu.VMEM((NZ, DIM, ROWS), bf16),
            pltpu.VMEM((NZ, ROWS, SPAN), bf16),
            pltpu.VMEM((PLANE, TILES, BAGS, DIM), bf16),
            pltpu.VMEM((NZ, PLANE, DIM, BAGS), bf16),
            pltpu.VMEM((PLANE, NZ, BAGS), i32),
            pltpu.VMEM((NZ, PLANE, LOOK, BAGS), i32),
            pltpu.VMEM((2, 4, 2, ROWS, HALF), bf16),
            pltpu.VMEM((2, 4, 2, ROWS, HALF), bf16),
            pltpu.VMEM((ROWS, DIM), f32),
            pltpu.VMEM((SPAN, DIM), bf16),
            pltpu.VMEM((FEAT, NX * ROWS), bf16),
            pltpu.VMEM((DIM, ROWS), bf16),
            pltpu.VMEM((DIM, BAGS), bf16),
            pltpu.SMEM((PLANE, NZ, BAGS), i32),
        ]
        + [dma(s) for s in sems],
        compiler_params=pltpu.CompilerParams(collective_id=0, has_side_effects=True, vmem_limit_bytes=58 << 20),
        name="move_rows_and_tiles",
    )(embedding.T, accumulator.T, msg, pooled_grad.reshape(TILES, BAGS, DIM))
    rows8 = ROWS // PLANE
    row_block = pl.BlockSpec((rows8, DIM), lambda i: (i, 0))
    pooled, new_rows, new_state = pl.pallas_call(
        finish_kernel,
        grid=(PLANE,),
        out_shape=(
            jax.ShapeDtypeStruct((TILES, BAGS, DIM), bf16),
            jax.ShapeDtypeStruct((ROWS, DIM), bf16),
            jax.ShapeDtypeStruct((ROWS, DIM), f32),
        ),
        in_specs=[smem, pl.BlockSpec((1, NZ, DIM, BAGS), lambda i: (i, 0, 0, 0)), row_block, row_block, row_block],
        out_specs=(pl.BlockSpec((TILES, BAGS, DIM), lambda i: (0, 0, 0)), row_block, row_block),
        scratch_shapes=[pltpu.VMEM((TILES, DIM, BAGS), f32)],
        compiler_params=pltpu.CompilerParams(vmem_limit_bytes=24 << 20),
        name="finish",
    )(tiles, arr, grad, own, state)
    return (pooled.reshape(TILES * BAGS, DIM), new_rows, new_state)


def solution(mesh):
    return jax.shard_map(
        per_device,
        mesh=mesh,
        in_specs=(
            P("table", "col"),
            P("table", "col"),
            P(("table", "col"), None, None),
            P(("table", "col"), None),
            P(("table", "col"), None),
            P(("table", "col"), None),
            P(("table", "col"), None),
        ),
        out_specs=(P(("table", "col"), None), P(("table", "col"), None), P(("table", "col"), None)),
        check_vma=False,
    )
```

```python
import functools
import jax
import jax.numpy as jnp
from jax import lax
from jax.experimental import pallas as pl
from jax.experimental.pallas import tpu as pltpu
from jax.sharding import PartitionSpec as P

LEARN_RATE = 0.3
EPSILON = 1e-08
MESH = pl.DeviceIdType.MESH
NY, NZ, NCORE, NX = 4, 8, 2, 4
PLANE = NY * NCORE
ROWS = 1024
DIM = 256
BAGS = 128
LOOK = 4
TILES = 16
FEAT = DIM // NX
SPAN = PLANE * BAGS
TILE_UNIT = 2048
PAIRS = NZ * PLANE
HALF = DIM // 2


def move_kernel(
    emb_ref, acc_ref, cot_ref, lens_ref, rows_ref, dest_ref, tile_ref,
    arr_ref, tiles_ref, grad_ref, own_ref, state_ref,
    emb_all, counts, cot_all, part, tile_rows, idx, msg, gsend, grecv, gsum, chosen, acc_half, acc_own, row_ids, tile_nums,
    acc_full, lens, pair_rows, dests, pair_tiles,
    ex_s, ex_r, ax_s, ax_r, ix_s, ix_r, e_s, e_r, cy_s, cy_r, cx_s, cx_r, p_s, p_r, t_s, t_r, g_s, g_r, loc,
):
    t = lax.axis_index("table")
    x = lax.axis_index("col")
    y, z, core = t // (NZ * NCORE), (t // NCORE) % NZ, t % NCORE

    def at(yy, zz, cc):
        return (lax.rem(yy + NY, NY) * NZ + lax.rem(zz + NZ, NZ)) * NCORE + lax.rem(cc + NCORE, NCORE)

    def plane(zz):
        return lax.rem(zz + 2 * NZ, NZ)

    def spot(yy, cc):
        return lax.rem(yy + NY, NY) * NCORE + lax.rem(cc + NCORE, NCORE)

    me = spot(y, core)
    others = [(dy, dc) for dy in (2, 1, 3, 0) for dc in (0, 1) if (dy, dc) != (0, 0)]

    barrier = pltpu.get_barrier_semaphore()
    for j in range(1, NX):
        pl.semaphore_signal(barrier, inc=1, device_id=(t, lax.rem(x + j, NX)), device_id_type=MESH)
    for j in range(1, NZ):
        pl.semaphore_signal(barrier, inc=1, device_id=(at(y, z + j, core), x), device_id_type=MESH)
    for dy, dc in others:
        pl.semaphore_signal(barrier, inc=1, device_id=(at(y + dy, z, core + dc), x), device_id_type=MESH)

    def local(src, dst, k):
        copy = pltpu.make_async_copy(src, dst, loc.at[k])
        copy.start()
        return copy

    def feature_rows(q):
        return pl.ds(pl.multiple_of(q * FEAT, FEAT), FEAT)

    def lanes(start, size):
        return pl.ds(pl.multiple_of(start, 128), size)

    small = [
        local(rows_ref, pair_rows, 10), local(lens_ref, lens, 11),
        local(dest_ref, dests, 12), local(tile_ref, pair_tiles, 13),
    ]
    own_rows = local(emb_ref.at[:, lanes(x * ROWS, ROWS)], emb_all.at[z, feature_rows(x)], 14)
    acc_in = local(acc_ref, acc_full, 15)
    own_cot = local(cot_ref, cot_all.at[me], 0)
    pl.semaphore_wait(barrier, NX - 1 + NZ - 1 + PLANE - 1)

    sent = []

    def send(src, dst, send_sem, recv_sem, table, col):
        copy = pltpu.make_async_remote_copy(
            src_ref=src, dst_ref=dst, send_sem=send_sem, recv_sem=recv_sem, device_id=(table, col), device_id_type=MESH
        )
        copy.start()
        sent.append(copy)

    def arrived(dst, recv_sem):
        pltpu.make_async_copy(dst, dst, recv_sem).wait()

    for j in (1, 3, 2):
        owner = lax.rem(x + j, NX)
        send(
            emb_ref.at[:, lanes(owner * ROWS, ROWS)], emb_all.at[z, feature_rows(x)],
            ex_s.at[j - 1], ex_r.at[j - 1], t, owner,
        )

    ORDER = (0, 1, 3, 2)

    def pass_rows(way, step, order, q):
        source = plane(z - step) if way == 0 else plane(z + step)
        target = plane(z + 1) if way == 0 else plane(z - 1)
        block = emb_all.at[source, feature_rows(q)]
        send(block, block, e_s.at[way, step, order], e_r.at[way, step + 1, order], at(y, target, core), x)

    def wait_rows(way, step, order, q):
        source = plane(z - step) if way == 0 else plane(z + step)
        arrived(emb_all.at[source, feature_rows(q)], e_r.at[way, step, order])

    own_rows.wait()
    for way in (0, 1):
        pass_rows(way, 0, 0, x)

    def tiles4(c):
        return pl.ds(4 * c, 4)

    for c in range(4):
        for way, dy in ((0, 1), (1, -1)):
            c_way = c if way == 0 else (c + 2) % 4
            send(
                cot_ref.at[tiles4(c_way)], cot_all.at[me, tiles4(c_way)],
                cy_s.at[way, 0, c_way], cy_r.at[way, 1, c_way], at(y + dy, z, core), x,
            )
    for c in range(4):
        send(cot_ref.at[tiles4(c)], cot_all.at[me, tiles4(c)], cx_s.at[0, c], cx_r.at[0, c], at(y, z, core + 1), x)

    for copy in small:
        copy.wait()
    place = lax.broadcasted_iota(jnp.int32, (PAIRS, PAIRS), 0)
    where_to = ((place & 7) >> 1) * (NZ * NCORE) + (place >> 3) * NCORE + (place & 1)
    match = dests[...] == where_to
    pick_pair = jnp.where(match, 1.0, 0.0).astype(jnp.bfloat16)
    pair_tile = jnp.sum(jnp.where(match, pair_tiles[...], 0), axis=1, keepdims=True)
    for l in range(LOOK):
        row = jnp.where(lens[...] > l, pair_rows[:, l, :], ROWS)
        high = (row >> 5).astype(jnp.float32).astype(jnp.bfloat16)
        low = (row & 31).astype(jnp.float32).astype(jnp.bfloat16)
        got = jnp.dot(pick_pair, high, preferred_element_type=jnp.float32) * 32.0 + jnp.dot(
            pick_pair, low, preferred_element_type=jnp.float32
        )
        msg[:, l] = (got.astype(jnp.int32) + pair_tile * TILE_UNIT).reshape(NZ, PLANE, BAGS)
    for off in (1, 7, 2, 6, 3, 5, 4):
        target = plane(z + off)
        send(msg.at[target], idx.at[z], ix_s.at[off], ix_r.at[off], at(y, target, core), x)
    idx[z] = msg[z]

    ids = lax.broadcasted_iota(jnp.int32, (DIM, BAGS), 0)
    row_ids[...] = ids.astype(jnp.float32).astype(jnp.bfloat16)

    def build(zo):
        one, zero = jnp.ones((), jnp.bfloat16), jnp.zeros((), jnp.bfloat16)

        def pair(n, carry):
            held = [idx[zo, l, pl.ds(n, 1), :] for l in range(LOOK)]
            tile_rows[n, pl.ds(zo, 1), :] = (held[0] >> 11) & (TILES - 1)
            for block in range(ROWS // DIM):
                total = None
                for l in range(LOOK):
                    near = jnp.clip((held[l] & (TILE_UNIT - 1)) - block * DIM, -1, DIM)
                    hit = jnp.where(row_ids[...] == near.astype(jnp.float32).astype(jnp.bfloat16), one, zero)
                    total = hit if total is None else total + hit
                counts[zo, pl.ds(block * DIM, DIM), lanes(n * BAGS, BAGS)] = total
            return carry

        lax.fori_loop(0, PLANE, pair, 0)

    def pool(zo):
        def block(b, carry):
            got = jnp.dot(
                emb_all[zo], counts[zo, :, lanes(b * DIM, DIM)], preferred_element_type=jnp.float32
            ).astype(jnp.bfloat16)
            part[zo, 2 * b] = got[:, :BAGS]
            part[zo, 2 * b + 1] = got[:, BAGS:]
            return carry

        lax.fori_loop(0, SPAN // DIM, block, 0)

    kept = []

    def send_part(zo, order):
        for k, (dy, dc) in enumerate(others):
            dest = spot(y + dy, core + dc)
            send(part.at[zo, dest], arr_ref.at[me, zo], p_s.at[order, k], p_r.at[order, k], at(y + dy, z, core + dc), x)
        kept.append(local(part.at[zo, me], arr_ref.at[me, zo], 1 + order))

    def relay_cot(way, step, c):
        dy = 1 if way == 0 else -1
        source = spot(y - dy * step, core)
        block = cot_all.at[source, tiles4(c)]
        arrived(block, cy_r.at[way, step, c])
        if step == 1 and c // 2 == way:
            send(block, block, cy_s.at[way, 1, c], cy_r.at[way, 2, c], at(y + dy, z, core), x)
        slot = 1 + way if step == 1 else 3
        send(block, block, cx_s.at[slot, c], cx_r.at[slot, c], at(y, z, core + 1), x)

    def gradient(zo, slot):
        def pick(n, carry):
            chosen[pl.ds(pl.multiple_of(n * BAGS, BAGS), BAGS), :] = cot_all[n, tile_nums[n, zo, 0]]
            return carry

        lax.fori_loop(0, PLANE, pick, 0)

        def block(b, carry):
            rows = pl.ds(pl.multiple_of(b * DIM, DIM), DIM)
            gsum[slot, rows, :] = jnp.dot(counts[zo, rows, :], chosen[...], preferred_element_type=jnp.float32)
            return carry

        lax.fori_loop(0, ROWS // DIM, block, 0)

    def pass_grad(way, dist, block, add, slot):
        rows = slice(block * DIM, (block + 1) * DIM)
        value = gsum[slot, rows, :]
        if add:
            arrived(grecv.at[way, dist, rows], g_r.at[way, dist, block])
            value = value + grecv[way, dist, rows, :].astype(jnp.float32)
        gsend[way, dist - 1, rows, :] = value.astype(jnp.bfloat16)
        target = plane(z + 1) if way == 0 else plane(z - 1)
        send(
            gsend.at[way, dist - 1, rows], grecv.at[way, dist - 1, rows],
            g_s.at[way, dist - 1, block], g_r.at[way, dist - 1, block], at(y, target, core), x,
        )

    zs = [z] + [plane(z - s) if w == 0 else plane(z + s) for s in (1, 2, 3) for w in (0, 1)] + [plane(z + 4)]

    def builds(step):
        for way in (0, 1) if step < 4 else (0,):
            zo = plane(z - step) if way == 0 else plane(z + step)
            arrived(idx.at[zo], ix_r.at[step if way == 0 else NZ - step])
            build(zo)

    def rows_on(step):
        for k in range(NX):
            q = lax.rem(x - ORDER[k] + NX, NX)
            for way in (0, 1):
                wait_rows(way, step, k, q)
                if step < 3 or (k < 2) == (way == 0):
                    pass_rows(way, step, k, q)

    build(z)
    for k in range(1, NX):
        j = ORDER[k]
        q = lax.rem(x - j + NX, NX)
        arrived(emb_all.at[z, feature_rows(q)], ex_r.at[j - 1])
        for way in (0, 1):
            pass_rows(way, 0, k, q)
    acc_in.wait()
    acc_half[...] = acc_full[...].astype(jnp.bfloat16)
    for j in range(1, NX):
        owner = lax.rem(x + j, NX)
        send(
            acc_half.at[:, lanes(owner * ROWS, ROWS)], acc_own.at[feature_rows(x)],
            ax_s.at[j - 1], ax_r.at[j - 1], t, owner,
        )
    acc_own[feature_rows(x), :] = acc_half[:, lanes(x * ROWS, ROWS)]
    builds(1)
    rows_on(1)
    for c in (0, 1):
        relay_cot(0, 1, c)
        relay_cot(1, 1, 2 + c)
    pool(z)
    builds(2)
    rows_on(2)
    for c in (0, 1):
        relay_cot(0, 1, 2 + c)
        relay_cot(1, 1, c)
    pool(zs[1])
    pool(zs[2])
    builds(3)
    for c in (0, 1):
        relay_cot(0, 2, c)
        relay_cot(1, 2, 2 + c)
    for order in (0, 1, 2):
        send_part(zs[order], order)
    rows_on(3)
    builds(4)

    to_scalars = local(tile_rows, tile_nums, 9)
    for k, (dy, dc) in enumerate(others):
        dest = spot(y + dy, core + dc)
        send(tile_rows.at[dest], tiles_ref.at[me], t_s.at[k], t_r.at[k], at(y + dy, z, core + dc), x)
    tiles_ref[me] = tile_rows[me]
    to_scalars.wait()

    own_cot.wait()
    for c in range(4):
        arrived(cot_all.at[spot(y, core + 1), tiles4(c)], cx_r.at[0, c])
        arrived(cot_all.at[spot(y - 1, core + 1), tiles4(c)], cx_r.at[1, c])
        arrived(cot_all.at[spot(y + 1, core + 1), tiles4(c)], cx_r.at[2, c])
        arrived(cot_all.at[spot(y + 2, core + 1), tiles4(c)], cx_r.at[3, c])

    gradient(zs[7], 0)
    for block in (0, 1):
        pass_grad(0, 4, block, False, 0)
        pass_grad(1, 4, block + 2, False, 0)
    for order in (3, 4):
        pool(zs[order])
        send_part(zs[order], order)
    early, late = ((2, 3), (0, 1)), ((0, 1), (2, 3))
    for dist in (3, 2, 1):
        for way in (0, 1):
            gradient(plane(z + dist) if way == 0 else plane(z - dist), way)
        if dist == 2:
            for order in (5, 6):
                pool(zs[order])
                send_part(zs[order], order)
        if dist == 1:
            for k in range(NX):
                wait_rows(0 if k < 2 else 1, 4, k, lax.rem(x - ORDER[k] + NX, NX))
            pool(zs[7])
            send_part(zs[7], 7)
        for blocks, add in ((early, dist < 3), (late, True)):
            for k in (0, 1):
                for way in (0, 1):
                    pass_grad(way, dist, blocks[way][k], add, way)
    gradient(z, 0)

    for j in range(1, NX):
        arrived(acc_own.at[feature_rows(lax.rem(x - j + NX, NX))], ax_r.at[j - 1])

    def turn(b, carry):
        rows = pl.ds(pl.multiple_of(b * 128, 128), 128)
        own_ref[rows, :] = emb_all[z, :, rows].astype(jnp.float32).T.astype(jnp.bfloat16)
        state_ref[rows, :] = acc_own[:, rows].astype(jnp.float32).T.astype(jnp.bfloat16)
        return carry

    lax.fori_loop(0, ROWS // 128, turn, 0)

    for way in (0, 1):
        for block in range(ROWS // DIM):
            arrived(grecv.at[way, 0, block * DIM : (block + 1) * DIM], g_r.at[way, 0, block])

    def total(b, carry):
        rows = pl.ds(pl.multiple_of(b * DIM, DIM), DIM)
        grad_ref[rows, :] = (
            gsum[0, rows, :] + grecv[0, 0, rows, :].astype(jnp.float32) + grecv[1, 0, rows, :].astype(jnp.float32)
        )
        return carry

    lax.fori_loop(0, ROWS // DIM, total, 0)

    for order, zo in enumerate(zs):
        for k, (dy, dc) in enumerate(others):
            arrived(arr_ref.at[spot(y - dy, core - dc), zo], p_r.at[order, k])
    for k, (dy, dc) in enumerate(others):
        arrived(tiles_ref.at[spot(y - dy, core - dc)], t_r.at[k])
    for copy in kept:
        copy.wait()
    for copy in sent:
        copy.wait_send()


def finish_kernel(tiles_ref, arr_ref, grad_ref, own_ref, state_ref, pooled_ref, rows_ref, sums_ref, total):
    step = pl.program_id(0)

    @pl.when(step == 0)
    def _():
        total[...] = jnp.zeros_like(total)

    def add(k, carry):
        tile = tiles_ref[step, k, 0]
        total[tile] = total[tile] + arr_ref[0, k].astype(jnp.float32)
        return carry

    lax.fori_loop(0, NZ, add, 0)
    grad = grad_ref[...]
    new_state = state_ref[...].astype(jnp.float32) + grad * grad
    sums_ref[...] = new_state
    rows_ref[...] = (
        own_ref[...].astype(jnp.float32) - LEARN_RATE * grad / (jnp.sqrt(new_state) + EPSILON)
    ).astype(jnp.bfloat16)

    @pl.when(step == PLANE - 1)
    def _():
        def turn(k, carry):
            pooled_ref[k] = total[k].T.astype(jnp.bfloat16)
            return carry

        lax.fori_loop(0, TILES, turn, 0)


def per_device(embedding, accumulator, pair_rows, pair_len, pair_dest, pair_tile, pooled_grad):
    smem = pl.BlockSpec(memory_space=pltpu.SMEM)
    vmem = pl.BlockSpec(memory_space=pltpu.VMEM)
    hbm = pl.BlockSpec(memory_space=pl.ANY)
    bf16, f32, i32 = jnp.bfloat16, jnp.float32, jnp.int32
    dma = pltpu.SemaphoreType.DMA
    sems = [(3,), (3,), (3,), (3,), (8,), (8,), (2, 5, 4), (2, 5, 4), (2, 3, 4), (2, 3, 4), (4, 4), (4, 4),
            (8, 7), (8, 7), (7,), (7,), (2, 4, 4), (2, 4, 4), (16,)]
    arr, tiles, grad, own, state = pl.pallas_call(
        move_kernel,
        out_shape=(
            jax.ShapeDtypeStruct((PLANE, NZ, DIM, BAGS), bf16),
            jax.ShapeDtypeStruct((PLANE, NZ, BAGS), i32),
            jax.ShapeDtypeStruct((ROWS, DIM), f32),
            jax.ShapeDtypeStruct((ROWS, DIM), bf16),
            jax.ShapeDtypeStruct((ROWS, DIM), bf16),
        ),
        in_specs=[hbm] * 7,
        out_specs=(hbm, vmem, vmem, vmem, vmem),
        scratch_shapes=[
            pltpu.VMEM((NZ, DIM, ROWS), bf16),
            pltpu.VMEM((NZ, ROWS, SPAN), bf16),
            pltpu.VMEM((PLANE, TILES, BAGS, DIM), bf16),
            pltpu.VMEM((NZ, PLANE, DIM, BAGS), bf16),
            pltpu.VMEM((PLANE, NZ, BAGS), i32),
            pltpu.VMEM((NZ, LOOK, PLANE, BAGS), i32),
            pltpu.VMEM((NZ, LOOK, PLANE, BAGS), i32),
            pltpu.VMEM((2, 4, ROWS, DIM), bf16),
            pltpu.VMEM((2, 4, ROWS, DIM), bf16),
            pltpu.VMEM((2, ROWS, DIM), f32),
            pltpu.VMEM((SPAN, DIM), bf16),
            pltpu.VMEM((FEAT, NX * ROWS), bf16),
            pltpu.VMEM((DIM, ROWS), bf16),
            pltpu.VMEM((DIM, BAGS), bf16),
            pltpu.SMEM((PLANE, NZ, BAGS), i32),
            pltpu.VMEM((FEAT, NX * ROWS), f32),
            pltpu.VMEM((PAIRS, BAGS), i32),
            pltpu.VMEM((PAIRS, LOOK, BAGS), i32),
            pltpu.VMEM((1, PAIRS), i32),
            pltpu.VMEM((1, PAIRS), i32),
        ]
        + [dma(s) for s in sems],
        compiler_params=pltpu.CompilerParams(collective_id=0, has_side_effects=True, vmem_limit_bytes=58 << 20),
        name="move_rows_and_tiles",
    )(
        embedding.T, accumulator.T, pooled_grad.reshape(TILES, BAGS, DIM),
        pair_len, jnp.transpose(pair_rows, (0, 2, 1)), pair_dest, pair_tile,
    )
    rows8 = ROWS // PLANE
    row_block = pl.BlockSpec((rows8, DIM), lambda i: (i, 0))
    pooled, new_rows, new_state = pl.pallas_call(
        finish_kernel,
        grid=(PLANE,),
        out_shape=(
            jax.ShapeDtypeStruct((TILES, BAGS, DIM), bf16),
            jax.ShapeDtypeStruct((ROWS, DIM), bf16),
            jax.ShapeDtypeStruct((ROWS, DIM), f32),
        ),
        in_specs=[smem, pl.BlockSpec((1, NZ, DIM, BAGS), lambda i: (i, 0, 0, 0)), row_block, row_block, row_block],
        out_specs=(pl.BlockSpec((TILES, BAGS, DIM), lambda i: (0, 0, 0)), row_block, row_block),
        scratch_shapes=[pltpu.VMEM((TILES, DIM, BAGS), f32)],
        compiler_params=pltpu.CompilerParams(vmem_limit_bytes=58 << 20),
        name="finish",
    )(tiles, arr, grad, own, state)
    return (pooled.reshape(TILES * BAGS, DIM), new_rows, new_state)


def solution(mesh):
    return jax.shard_map(
        per_device,
        mesh=mesh,
        in_specs=(
            P("table", "col"),
            P("table", "col"),
            P(("table", "col"), None, None),
            P(("table", "col"), None),
            P(("table", "col"), None),
            P(("table", "col"), None),
            P(("table", "col"), None),
        ),
        out_specs=(P(("table", "col"), None), P(("table", "col"), None), P(("table", "col"), None)),
        check_vma=False,
    )
```

```python
import functools
import jax
import jax.numpy as jnp
from jax import lax
from jax.experimental import pallas as pl
from jax.experimental.pallas import tpu as pltpu
from jax.sharding import PartitionSpec as P

LEARN_RATE = 0.3
EPSILON = 1e-08
MESH = pl.DeviceIdType.MESH
NY, NZ, NCORE, NX = 4, 8, 2, 4
PLANE = NY * NCORE
ROWS = 1024
DIM = 256
BAGS = 128
LOOK = 4
TILES = 16
FEAT = DIM // NX
SPAN = PLANE * BAGS
TILE_UNIT = 2048
PAIRS = NZ * PLANE
HALF = DIM // 2


def move_kernel(
    emb_ref, acc_ref, cot_ref, lens_ref, rows_ref, dest_ref, tile_ref,
    pooled_ref, new_rows_ref, new_sums_ref,
    emb_all, counts, cot_all, part, tile_rows, idx, msg, gfar, grecv, gsum, chosen, acc_half, acc_own, row_ids, tile_nums,
    acc_full, lens, pair_rows, dests, pair_tiles, arr, tiles, sums, codes, code_nums, pooled, grad, own, state,
    ex_s, ex_r, ax_s, ax_r, ix_s, ix_r, e_s, e_r, cy_s, cy_r, cx_s, cx_r, p_s, p_r, t_s, t_r, g_s, g_r, loc,
):
    t = lax.axis_index("table")
    x = lax.axis_index("col")
    y, z, core = t // (NZ * NCORE), (t // NCORE) % NZ, t % NCORE

    def at(yy, zz, cc):
        return (lax.rem(yy + NY, NY) * NZ + lax.rem(zz + NZ, NZ)) * NCORE + lax.rem(cc + NCORE, NCORE)

    def plane(zz):
        return lax.rem(zz + 2 * NZ, NZ)

    def spot(yy, cc):
        return lax.rem(yy + NY, NY) * NCORE + lax.rem(cc + NCORE, NCORE)

    me = spot(y, core)
    others = [(dy, dc) for dy in (2, 1, 3, 0) for dc in (0, 1) if (dy, dc) != (0, 0)]

    barrier = pltpu.get_barrier_semaphore()
    for j in range(1, NX):
        pl.semaphore_signal(barrier, inc=1, device_id=(t, lax.rem(x + j, NX)), device_id_type=MESH)
    for j in range(1, NZ):
        pl.semaphore_signal(barrier, inc=1, device_id=(at(y, z + j, core), x), device_id_type=MESH)
    for dy, dc in others:
        pl.semaphore_signal(barrier, inc=1, device_id=(at(y + dy, z, core + dc), x), device_id_type=MESH)

    def local(src, dst, k):
        copy = pltpu.make_async_copy(src, dst, loc.at[k])
        copy.start()
        return copy

    def feature_rows(q):
        return pl.ds(pl.multiple_of(q * FEAT, FEAT), FEAT)

    def lanes(start, size):
        return pl.ds(pl.multiple_of(start, 128), size)

    small = [
        local(rows_ref, pair_rows, 10), local(lens_ref, lens, 11),
        local(dest_ref, dests, 12), local(tile_ref, pair_tiles, 13),
    ]
    own_rows = local(emb_ref.at[:, lanes(x * ROWS, ROWS)], emb_all.at[z, feature_rows(x)], 14)
    acc_in = local(acc_ref, acc_full, 15)
    own_cot = local(cot_ref, cot_all.at[me], 0)
    pl.semaphore_wait(barrier, NX - 1 + NZ - 1 + PLANE - 1)

    sent = []

    def send(src, dst, send_sem, recv_sem, table, col):
        copy = pltpu.make_async_remote_copy(
            src_ref=src, dst_ref=dst, send_sem=send_sem, recv_sem=recv_sem, device_id=(table, col), device_id_type=MESH
        )
        copy.start()
        sent.append(copy)
        return copy

    def room(stream):
        if len(stream) == 2:
            first = stream.pop(0)
            first.wait_send()
            sent[:] = [copy for copy in sent if copy is not first]

    def arrived(dst, recv_sem):
        pltpu.make_async_copy(dst, dst, recv_sem).wait()

    for j in (1, 3, 2):
        owner = lax.rem(x + j, NX)
        send(
            emb_ref.at[:, lanes(owner * ROWS, ROWS)], emb_all.at[z, feature_rows(x)],
            ex_s.at[j - 1], ex_r.at[j - 1], t, owner,
        )

    ORDER = (0, 1, 3, 2)

    def pass_rows(way, step, order, q):
        source = plane(z - step) if way == 0 else plane(z + step)
        target = plane(z + 1) if way == 0 else plane(z - 1)
        block = emb_all.at[source, feature_rows(q)]
        return send(block, block, e_s.at[way, step, order], e_r.at[way, step + 1, order], at(y, target, core), x)

    def wait_rows(way, step, order, q):
        source = plane(z - step) if way == 0 else plane(z + step)
        arrived(emb_all.at[source, feature_rows(q)], e_r.at[way, step, order])

    row_stream, cot_stream, grad_stream = ([], []), ([], []), ([], [])

    def rows_step(i):
        step, k = i // NX, i % NX
        if i == 0:
            own_rows.wait()
        elif step == 0:
            arrived(emb_all.at[z, feature_rows(lax.rem(x - ORDER[k] + NX, NX))], ex_r.at[ORDER[k] - 1])
        for way in (0, 1):
            kk = k + 2 * way if step == 3 else k
            q = lax.rem(x - ORDER[kk] + NX, NX)
            if step:
                wait_rows(way, step, kk, q)
            room(row_stream[way])
            row_stream[way].append(pass_rows(way, step, kk, q))

    rows_step(0)

    def tiles4(c):
        return pl.ds(4 * c, 4)

    def send_cot(c):
        for way, dy in ((0, 1), (1, -1)):
            c_way = c if way == 0 else (c + 2) % 4
            room(cot_stream[way])
            cot_stream[way].append(
                send(
                    cot_ref.at[tiles4(c_way)], cot_all.at[me, tiles4(c_way)],
                    cy_s.at[way, 0, c_way], cy_r.at[way, 1, c_way], at(y + dy, z, core), x,
                )
            )

    send_cot(0)

    for copy in small:
        copy.wait()
    place = lax.broadcasted_iota(jnp.int32, (PAIRS, PAIRS), 0)
    where_to = ((place & 7) >> 1) * (NZ * NCORE) + (place >> 3) * NCORE + (place & 1)
    match = dests[...] == where_to
    pick_pair = jnp.where(match, 1.0, 0.0).astype(jnp.bfloat16)
    pair_tile = jnp.sum(jnp.where(match, pair_tiles[...], 0), axis=1, keepdims=True)
    for l in range(LOOK):
        row = jnp.where(lens[...] > l, pair_rows[:, l, :], ROWS)
        high = (row >> 5).astype(jnp.float32).astype(jnp.bfloat16)
        low = (row & 31).astype(jnp.float32).astype(jnp.bfloat16)
        got = jnp.dot(pick_pair, high, preferred_element_type=jnp.float32) * 32.0 + jnp.dot(
            pick_pair, low, preferred_element_type=jnp.float32
        )
        msg[:, l] = (got.astype(jnp.int32) + pair_tile * TILE_UNIT).reshape(NZ, PLANE, BAGS)
    for off in (1, 7, 2, 6, 3, 5, 4):
        target = plane(z + off)
        send(msg.at[target], idx.at[z], ix_s.at[off], ix_r.at[off], at(y, target, core), x)
    idx[z] = msg[z]

    ids = lax.broadcasted_iota(jnp.int32, (DIM, BAGS), 0)
    row_ids[...] = ids.astype(jnp.float32).astype(jnp.bfloat16)

    def build(zo, order):
        one, zero = jnp.ones((), jnp.bfloat16), jnp.zeros((), jnp.bfloat16)

        def pair(n, carry):
            held = [idx[zo, l, pl.ds(n, 1), :] for l in range(LOOK)]
            tile_rows[n, order : order + 1, :] = (held[0] >> 11) & (TILES - 1)
            for block in range(ROWS // DIM):
                total = None
                for l in range(LOOK):
                    near = jnp.clip((held[l] & (TILE_UNIT - 1)) - block * DIM, -1, DIM)
                    hit = jnp.where(row_ids[...] == near.astype(jnp.float32).astype(jnp.bfloat16), one, zero)
                    total = hit if total is None else total + hit
                counts[zo, pl.ds(block * DIM, DIM), lanes(n * BAGS, BAGS)] = total
            return carry

        lax.fori_loop(0, PLANE, pair, 0)

    def pool(zo):
        def block(b, carry):
            got = jnp.dot(
                emb_all[zo], counts[zo, :, lanes(b * DIM, DIM)], preferred_element_type=jnp.float32
            ).astype(jnp.bfloat16)
            part[zo, 2 * b] = got[:, :BAGS]
            part[zo, 2 * b + 1] = got[:, BAGS:]
            return carry

        lax.fori_loop(0, SPAN // DIM, block, 0)

    kept = []

    def send_part(order):
        zo = zs[order]
        for k, (dy, dc) in enumerate(others):
            dest = spot(y + dy, core + dc)
            send(part.at[zo, dest], arr.at[me, order], p_s.at[order, k], p_r.at[order, k], at(y + dy, z, core + dc), x)
        kept.append(local(part.at[zo, me], arr.at[me, order], 1 + order))

    def relay_cot(way, step, c):
        dy = 1 if way == 0 else -1
        source = spot(y - dy * step, core)
        block = cot_all.at[source, tiles4(c)]
        arrived(block, cy_r.at[way, step, c])
        if step == 1 and c // 2 == way:
            room(cot_stream[way])
            cot_stream[way].append(
                send(block, block, cy_s.at[way, 1, c], cy_r.at[way, 2, c], at(y + dy, z, core), x)
            )
        slot = 1 + way if step == 1 else 3
        send(block, block, cx_s.at[slot, c], cx_r.at[slot, c], at(y, z, core + 1), x)

    def gradient(order, slot):
        zo = zs[order]
        into = grad if slot is None else gsum.at[slot]

        def pick(n, carry):
            chosen[pl.ds(pl.multiple_of(n * BAGS, BAGS), BAGS), :] = cot_all[n, tile_nums[n, order, 0]]
            return carry

        lax.fori_loop(0, PLANE, pick, 0)

        def block(b, carry):
            rows = pl.ds(pl.multiple_of(b * DIM, DIM), DIM)
            into[rows, :] = jnp.dot(counts[zo, rows, :], chosen[...], preferred_element_type=jnp.float32)
            return carry

        lax.fori_loop(0, ROWS // DIM, block, 0)

    def pass_grad(way, dist, block, slot):
        rows = slice(block * DIM, (block + 1) * DIM)
        add = dist < 3 or (dist == 3 and (block < 2) == (way == 0))
        held = gfar.at[way] if dist == 4 else grecv.at[way, dist]
        value = gsum[slot, rows, :]
        if add:
            arrived(held.at[rows], g_r.at[way, dist, block])
            value = value + held[rows, :].astype(jnp.float32)
        room(grad_stream[way])
        spot_rows = rows if dist < 4 else slice(block % 2 * DIM, (block % 2 + 1) * DIM)
        held[spot_rows, :] = value.astype(jnp.bfloat16)
        target = plane(z + 1) if way == 0 else plane(z - 1)
        grad_stream[way].append(
            send(
                held.at[spot_rows], grecv.at[way, dist - 1, rows],
                g_s.at[way, dist - 1, block], g_r.at[way, dist - 1, block], at(y, target, core), x,
            )
        )

    early, late = ((2, 3), (0, 1)), ((0, 1), (2, 3))
    grad_steps = [(dist, blocks, k) for dist, blocks in (
        (4, late), (3, early), (3, late), (2, early), (2, late), (1, early), (1, late)
    ) for k in (0, 1)]

    def grads_step(i):
        dist, blocks, k = grad_steps[i]
        for way in (0, 1):
            pass_grad(way, dist, blocks[way][k], way if dist < 4 else 0)

    zs = [z] + [plane(z - s) if w == 0 else plane(z + s) for s in (1, 2, 3) for w in (0, 1)] + [plane(z + 4)]

    def build_next(order):
        arrived(idx.at[zs[order]], ix_r.at[(order + 1) // 2 if order % 2 else NZ - (order + 1) // 2])
        build(zs[order], order)

    def move_acc():
        acc_in.wait()
        acc_half[...] = acc_full[...].astype(jnp.bfloat16)
        for j in range(1, NX):
            owner = lax.rem(x + j, NX)
            send(
                acc_half.at[:, lanes(owner * ROWS, ROWS)], acc_own.at[feature_rows(x)],
                ax_s.at[j - 1], ax_r.at[j - 1], t, owner,
            )
        acc_own[feature_rows(x), :] = acc_half[:, lanes(x * ROWS, ROWS)]

    rows_step(1)
    send_cot(1)
    for c in range(4):
        send(cot_ref.at[tiles4(c)], cot_all.at[me, tiles4(c)], cx_s.at[0, c], cx_r.at[0, c], at(y, z, core + 1), x)
    build(z, 0)
    rows_step(2)
    move_acc()
    rows_step(3)
    send_cot(2)
    build_next(1)
    rows_step(4)
    pool(zs[0])
    send_part(0)
    rows_step(5)
    send_cot(3)
    build_next(2)
    rows_step(6)
    build_next(3)
    rows_step(7)
    relay_cot(0, 1, 0)
    relay_cot(1, 1, 2)
    build_next(4)
    rows_step(8)
    relay_cot(0, 1, 2)
    relay_cot(1, 1, 0)
    pool(zs[1])
    rows_step(9)
    relay_cot(0, 1, 1)
    relay_cot(1, 1, 3)
    pool(zs[2])
    rows_step(10)
    relay_cot(0, 1, 3)
    relay_cot(1, 1, 1)
    build_next(7)
    rows_step(11)
    build_next(5)
    relay_cot(0, 2, 0)
    relay_cot(1, 2, 2)
    rows_step(12)
    build_next(6)
    pool(zs[3])
    rows_step(13)

    to_scalars = local(tile_rows, tile_nums, 9)
    for k, (dy, dc) in enumerate(others):
        dest = spot(y + dy, core + dc)
        send(tile_rows.at[dest], tiles.at[me], t_s.at[k], t_r.at[k], at(y + dy, z, core + dc), x)
    tiles[me] = tile_rows[me]
    relay_cot(0, 2, 1)
    relay_cot(1, 2, 3)
    for order in (1, 2, 3):
        send_part(order)
    to_scalars.wait()
    own_cot.wait()
    for c in range(4):
        arrived(cot_all.at[spot(y, core + 1), tiles4(c)], cx_r.at[0, c])
        arrived(cot_all.at[spot(y - 1, core + 1), tiles4(c)], cx_r.at[1, c])
        arrived(cot_all.at[spot(y + 1, core + 1), tiles4(c)], cx_r.at[2, c])
        arrived(cot_all.at[spot(y + 2, core + 1), tiles4(c)], cx_r.at[3, c])

    gradient(7, 0)
    grads_step(0)
    gradient(5, 1)
    grads_step(1)
    gradient(6, 0)
    grads_step(2)
    pool(zs[4])
    grads_step(3)
    send_part(4)
    for k in (0, 1):
        wait_rows(0, 3, k + 2, lax.rem(x - ORDER[k + 2] + NX, NX))
        wait_rows(1, 3, k, lax.rem(x - ORDER[k] + NX, NX))
    pool(zs[5])
    grads_step(4)
    pool(zs[6])
    grads_step(5)
    send_part(5)
    gradient(4, 0)
    gradient(3, 1)
    grads_step(6)
    send_part(6)

    for k, (dy, dc) in enumerate(others):
        arrived(tiles.at[spot(y - dy, core - dc)], t_r.at[k])
    held = tiles[...].reshape(PAIRS, BAGS)
    down = lax.broadcasted_iota(jnp.int32, (PAIRS, BAGS), 0)
    across = lax.broadcasted_iota(jnp.int32, (PAIRS, BAGS), 1)
    tile_line = jnp.sum(jnp.where(down == across, held, 0), axis=0, keepdims=True)
    turn_down = ((down & 7) << 3) + (down >> 3)
    turn_across = ((across & 7) << 3) + (across >> 3)

    def last_of(found, turn):
        last = jnp.max(jnp.where(found, turn, -1), axis=1, keepdims=True)
        return jnp.broadcast_to(jnp.where(last < 0, PAIRS, last), (last.shape[0], BAGS))

    codes[:PAIRS] = last_of((tile_line == held) & (turn_across < turn_down) & (across < PAIRS), turn_across)
    codes[PAIRS:] = last_of((tile_line == down[:TILES]) & (across[:TILES] < PAIRS), turn_across[:TILES])
    to_codes = local(codes, code_nums, 16)
    sums[PAIRS] = jnp.zeros((DIM, BAGS), jnp.float32)

    grads_step(7)
    for k in range(NX):
        wait_rows(0 if k < 2 else 1, 4, k, lax.rem(x - ORDER[k] + NX, NX))
    pool(zs[7])
    grads_step(8)
    send_part(7)
    grads_step(9)
    gradient(2, 0)
    gradient(1, 1)
    grads_step(10)

    for j in range(1, NX):
        arrived(acc_own.at[feature_rows(lax.rem(x - j + NX, NX))], ax_r.at[j - 1])

    def turn(b, carry):
        rows = pl.ds(pl.multiple_of(b * 128, 128), 128)
        own[rows, :] = emb_all[z, :, rows].astype(jnp.float32).T.astype(jnp.bfloat16)
        state[rows, :] = acc_own[:, rows].astype(jnp.float32).T.astype(jnp.bfloat16)
        return carry

    lax.fori_loop(0, ROWS // 128, turn, 0)
    grads_step(11)
    to_codes.wait()

    def fold(order):
        for k, (dy, dc) in enumerate(others):
            arrived(arr.at[spot(y - dy, core - dc), order], p_r.at[order, k])
        kept[order].wait()

        def one(n, carry):
            sums[order * PLANE + n] = arr[n, order].astype(jnp.float32) + sums[code_nums[n * NZ + order, 0]]
            return carry

        lax.fori_loop(0, PLANE, one, 0)

    gradient(0, None)
    fold(0)
    fold(1)
    grads_step(12)
    fold(2)
    grads_step(13)
    for order in range(3, NZ):
        fold(order)
    outs = []

    def pool_out(k, carry):
        pooled[k] = sums[code_nums[PAIRS + k, 0]].T.astype(jnp.bfloat16)
        return carry

    for quarter in range(4):
        lax.fori_loop(4 * quarter, 4 * quarter + 4, pool_out, 0)
        outs.append(local(pooled.at[tiles4(quarter)], pooled_ref.at[tiles4(quarter)], 25 + quarter))
    for block in range(ROWS // DIM):
        rows = slice(block * DIM, (block + 1) * DIM)
        for way in (0, 1):
            arrived(grecv.at[way, 0, rows], g_r.at[way, 0, block])
        got = grad[rows, :] + grecv[0, 0, rows, :].astype(jnp.float32) + grecv[1, 0, rows, :].astype(jnp.float32)
        new_state = state[rows, :].astype(jnp.float32) + got * got
        grad[rows, :] = new_state
        own[rows, :] = (
            own[rows, :].astype(jnp.float32) - LEARN_RATE * got / (jnp.sqrt(new_state) + EPSILON)
        ).astype(jnp.bfloat16)
        outs.append(local(grad.at[rows], new_sums_ref.at[rows], 17 + block))
        outs.append(local(own.at[rows], new_rows_ref.at[rows], 21 + block))
    for copy in outs:
        copy.wait()
    for copy in sent:
        copy.wait_send()


def per_device(embedding, accumulator, pair_rows, pair_len, pair_dest, pair_tile, pooled_grad):
    hbm = pl.BlockSpec(memory_space=pl.ANY)
    bf16, f32, i32 = jnp.bfloat16, jnp.float32, jnp.int32
    dma = pltpu.SemaphoreType.DMA
    sems = [(3,), (3,), (3,), (3,), (8,), (8,), (2, 5, 4), (2, 5, 4), (2, 3, 4), (2, 3, 4), (4, 4), (4, 4),
            (8, 7), (8, 7), (7,), (7,), (2, 4, 4), (2, 4, 4), (29,)]
    pooled, new_rows, new_state = pl.pallas_call(
        move_kernel,
        out_shape=(
            jax.ShapeDtypeStruct((TILES, BAGS, DIM), bf16),
            jax.ShapeDtypeStruct((ROWS, DIM), bf16),
            jax.ShapeDtypeStruct((ROWS, DIM), f32),
        ),
        in_specs=[hbm] * 7,
        out_specs=[hbm] * 3,
        scratch_shapes=[
            pltpu.VMEM((NZ, DIM, ROWS), bf16),
            pltpu.VMEM((NZ, ROWS, SPAN), bf16),
            pltpu.VMEM((PLANE, TILES, BAGS, DIM), bf16),
            pltpu.VMEM((NZ, PLANE, DIM, BAGS), bf16),
            pltpu.VMEM((PLANE, NZ, BAGS), i32),
            pltpu.VMEM((NZ, LOOK, PLANE, BAGS), i32),
            pltpu.VMEM((NZ, LOOK, PLANE, BAGS), i32),
            pltpu.VMEM((2, ROWS // 2, DIM), bf16),
            pltpu.VMEM((2, 4, ROWS, DIM), bf16),
            pltpu.VMEM((2, ROWS, DIM), f32),
            pltpu.VMEM((SPAN, DIM), bf16),
            pltpu.VMEM((FEAT, NX * ROWS), bf16),
            pltpu.VMEM((DIM, ROWS), bf16),
            pltpu.VMEM((DIM, BAGS), bf16),
            pltpu.SMEM((PLANE, NZ, BAGS), i32),
            pltpu.VMEM((FEAT, NX * ROWS), f32),
            pltpu.VMEM((PAIRS, BAGS), i32),
            pltpu.VMEM((PAIRS, LOOK, BAGS), i32),
            pltpu.VMEM((1, PAIRS), i32),
            pltpu.VMEM((1, PAIRS), i32),
            pltpu.VMEM((PLANE, NZ, DIM, BAGS), bf16),
            pltpu.VMEM((PLANE, NZ, BAGS), i32),
            pltpu.VMEM((PAIRS + 1, DIM, BAGS), f32),
            pltpu.VMEM((PAIRS + TILES, BAGS), i32),
            pltpu.SMEM((PAIRS + TILES, BAGS), i32),
            pltpu.VMEM((TILES, BAGS, DIM), bf16),
            pltpu.VMEM((ROWS, DIM), f32),
            pltpu.VMEM((ROWS, DIM), bf16),
            pltpu.VMEM((ROWS, DIM), bf16),
        ]
        + [dma(s) for s in sems],
        compiler_params=pltpu.CompilerParams(collective_id=0, has_side_effects=True, vmem_limit_bytes=60 << 20),
        name="move_rows_and_tiles",
    )(
        embedding.T, accumulator.T, pooled_grad.reshape(TILES, BAGS, DIM),
        pair_len, jnp.transpose(pair_rows, (0, 2, 1)), pair_dest, pair_tile,
    )
    return (pooled.reshape(TILES * BAGS, DIM), new_rows, new_state)


def solution(mesh):
    return jax.shard_map(
        per_device,
        mesh=mesh,
        in_specs=(
            P("table", "col"),
            P("table", "col"),
            P(("table", "col"), None, None),
            P(("table", "col"), None),
            P(("table", "col"), None),
            P(("table", "col"), None),
            P(("table", "col"), None),
        ),
        out_specs=(P(("table", "col"), None), P(("table", "col"), None), P(("table", "col"), None)),
        check_vma=False,
    )
```

```python
import functools
import jax
import jax.numpy as jnp
from jax import lax
from jax.experimental import pallas as pl
from jax.experimental.pallas import tpu as pltpu
from jax.sharding import PartitionSpec as P

LEARN_RATE = 0.3
EPSILON = 1e-08
MESH = pl.DeviceIdType.MESH
NY, NZ, NCORE, NX = 4, 8, 2, 4
PLANE = NY * NCORE
ROWS = 1024
DIM = 256
BAGS = 128
LOOK = 4
TILES = 16
FEAT = DIM // NX
SPAN = PLANE * BAGS
TILE_UNIT = 2048
PAIRS = NZ * PLANE
HALF = DIM // 2


def move_kernel(
    emb_ref, acc_ref, cot_ref, lens_ref, rows_ref, dest_ref, tile_ref,
    pooled_ref, new_rows_ref, new_sums_ref,
    emb_all, counts, cot_all, part, tile_rows, idx, msg, gfar, grecv, gsum, chosen, acc_half, acc_own, row_ids, tile_nums,
    acc_full, lens, pair_rows, dests, pair_tiles, arr, tiles, sums, codes, code_nums, pooled, grad, own, state,
    ex_s, ex_r, ax_s, ax_r, ix_s, ix_r, e_s, e_r, cy_s, cy_r, cx_s, cx_r, p_s, p_r, t_s, t_r, g_s, g_r, loc,
):
    t = lax.axis_index("table")
    x = lax.axis_index("col")
    y, z, core = t // (NZ * NCORE), (t // NCORE) % NZ, t % NCORE

    def at(yy, zz, cc):
        return (lax.rem(yy + NY, NY) * NZ + lax.rem(zz + NZ, NZ)) * NCORE + lax.rem(cc + NCORE, NCORE)

    def plane(zz):
        return lax.rem(zz + 2 * NZ, NZ)

    def spot(yy, cc):
        return lax.rem(yy + NY, NY) * NCORE + lax.rem(cc + NCORE, NCORE)

    me = spot(y, core)
    others = [(dy, dc) for dy in (2, 1, 3, 0) for dc in (0, 1) if (dy, dc) != (0, 0)]

    barrier = pltpu.get_barrier_semaphore()
    for j in range(1, NX):
        pl.semaphore_signal(barrier, inc=1, device_id=(t, lax.rem(x + j, NX)), device_id_type=MESH)
    for j in range(1, NZ):
        pl.semaphore_signal(barrier, inc=1, device_id=(at(y, z + j, core), x), device_id_type=MESH)
    for dy, dc in others:
        pl.semaphore_signal(barrier, inc=1, device_id=(at(y + dy, z, core + dc), x), device_id_type=MESH)

    def local(src, dst, k):
        copy = pltpu.make_async_copy(src, dst, loc.at[k])
        copy.start()
        return copy

    def feature_rows(q):
        return pl.ds(pl.multiple_of(q * FEAT, FEAT), FEAT)

    def lanes(start, size):
        return pl.ds(pl.multiple_of(start, 128), size)

    small = [
        local(rows_ref, pair_rows, 10), local(lens_ref, lens, 11),
        local(dest_ref, dests, 12), local(tile_ref, pair_tiles, 13),
    ]
    own_rows = local(emb_ref.at[:, lanes(x * ROWS, ROWS)], emb_all.at[z, feature_rows(x)], 14)
    acc_in = local(acc_ref, acc_full, 15)
    own_cot = local(cot_ref, cot_all.at[me], 0)
    pl.semaphore_wait(barrier, NX - 1 + NZ - 1 + PLANE - 1)

    sent = []

    def send(src, dst, send_sem, recv_sem, table, col):
        copy = pltpu.make_async_remote_copy(
            src_ref=src, dst_ref=dst, send_sem=send_sem, recv_sem=recv_sem, device_id=(table, col), device_id_type=MESH
        )
        copy.start()
        sent.append(copy)
        return copy

    def room(stream, most):
        if len(stream) == most:
            first = stream.pop(0)
            first.wait_send()
            sent[:] = [copy for copy in sent if copy is not first]

    def arrived(dst, recv_sem):
        pltpu.make_async_copy(dst, dst, recv_sem).wait()

    for j in (1, 3, 2):
        owner = lax.rem(x + j, NX)
        send(
            emb_ref.at[:, lanes(owner * ROWS, ROWS)], emb_all.at[z, feature_rows(x)],
            ex_s.at[j - 1], ex_r.at[j - 1], t, owner,
        )

    ORDER = (0, 1, 3, 2)

    def pass_rows(way, step, order, q):
        source = plane(z - step) if way == 0 else plane(z + step)
        target = plane(z + 1) if way == 0 else plane(z - 1)
        block = emb_all.at[source, feature_rows(q)]
        return send(block, block, e_s.at[way, step, order], e_r.at[way, step + 1, order], at(y, target, core), x)

    def wait_rows(way, step, order, q):
        source = plane(z - step) if way == 0 else plane(z + step)
        arrived(emb_all.at[source, feature_rows(q)], e_r.at[way, step, order])

    row_stream, cot_stream, grad_stream = ([], []), ([], []), ([], [])

    def rows_step(i):
        step, k = i // NX, i % NX
        if i == 0:
            own_rows.wait()
        elif step == 0:
            arrived(emb_all.at[z, feature_rows(lax.rem(x - ORDER[k] + NX, NX))], ex_r.at[ORDER[k] - 1])
        for way in (0, 1):
            kk = k + 2 * way if step == 3 else k
            q = lax.rem(x - ORDER[kk] + NX, NX)
            if step:
                wait_rows(way, step, kk, q)
            room(row_stream[way], 3)
            row_stream[way].append(pass_rows(way, step, kk, q))

    rows_step(0)

    def tiles4(c):
        return pl.ds(4 * c, 4)

    def send_cot(c):
        for way, dy in ((0, 1), (1, -1)):
            c_way = c if way == 0 else (c + 2) % 4
            room(cot_stream[way], 2)
            cot_stream[way].append(
                send(
                    cot_ref.at[tiles4(c_way)], cot_all.at[me, tiles4(c_way)],
                    cy_s.at[way, 0, c_way], cy_r.at[way, 1, c_way], at(y + dy, z, core), x,
                )
            )

    send_cot(0)

    for copy in small:
        copy.wait()
    place = lax.broadcasted_iota(jnp.int32, (PAIRS, PAIRS), 0)
    where_to = ((place & 7) >> 1) * (NZ * NCORE) + (place >> 3) * NCORE + (place & 1)
    match = dests[...] == where_to
    pick_pair = jnp.where(match, 1.0, 0.0).astype(jnp.bfloat16)
    pair_tile = jnp.sum(jnp.where(match, pair_tiles[...], 0), axis=1, keepdims=True)
    for l in range(LOOK):
        row = jnp.where(lens[...] > l, pair_rows[:, l, :], ROWS)
        high = (row >> 5).astype(jnp.float32).astype(jnp.bfloat16)
        low = (row & 31).astype(jnp.float32).astype(jnp.bfloat16)
        got = jnp.dot(pick_pair, high, preferred_element_type=jnp.float32) * 32.0 + jnp.dot(
            pick_pair, low, preferred_element_type=jnp.float32
        )
        msg[:, l] = (got.astype(jnp.int32) + pair_tile * TILE_UNIT).reshape(NZ, PLANE, BAGS)
    for off in (1, 7, 2, 6, 3, 5, 4):
        target = plane(z + off)
        send(msg.at[target], idx.at[z], ix_s.at[off], ix_r.at[off], at(y, target, core), x)
    idx[z] = msg[z]

    ids = lax.broadcasted_iota(jnp.int32, (DIM, BAGS), 0)
    row_ids[...] = ids.astype(jnp.float32).astype(jnp.bfloat16)

    def build(zo, order):
        one, zero = jnp.ones((), jnp.bfloat16), jnp.zeros((), jnp.bfloat16)

        def pair(n, carry):
            held = [idx[zo, l, pl.ds(n, 1), :] for l in range(LOOK)]
            tile_rows[n, order : order + 1, :] = (held[0] >> 11) & (TILES - 1)
            for block in range(ROWS // DIM):
                total = None
                for l in range(LOOK):
                    near = jnp.clip((held[l] & (TILE_UNIT - 1)) - block * DIM, -1, DIM)
                    hit = jnp.where(row_ids[...] == near.astype(jnp.float32).astype(jnp.bfloat16), one, zero)
                    total = hit if total is None else total + hit
                counts[zo, pl.ds(block * DIM, DIM), lanes(n * BAGS, BAGS)] = total
            return carry

        lax.fori_loop(0, PLANE, pair, 0)

    def pool(zo):
        def block(b, carry):
            got = jnp.dot(
                emb_all[zo], counts[zo, :, lanes(b * DIM, DIM)], preferred_element_type=jnp.float32
            ).astype(jnp.bfloat16)
            part[zo, 2 * b] = got[:, :BAGS]
            part[zo, 2 * b + 1] = got[:, BAGS:]
            return carry

        lax.fori_loop(0, SPAN // DIM, block, 0)

    def send_part(order):
        zo = zs[order]
        for k, (dy, dc) in enumerate(others):
            dest = spot(y + dy, core + dc)
            send(part.at[zo, dest], arr.at[me, order], p_s.at[order, k], p_r.at[order, k], at(y + dy, z, core + dc), x)
        arr[me, order] = part[zo, me]

    def relay_cot(way, step, c):
        dy = 1 if way == 0 else -1
        source = spot(y - dy * step, core)
        block = cot_all.at[source, tiles4(c)]
        arrived(block, cy_r.at[way, step, c])
        if step == 1 and c // 2 == way:
            room(cot_stream[way], 2)
            cot_stream[way].append(
                send(block, block, cy_s.at[way, 1, c], cy_r.at[way, 2, c], at(y + dy, z, core), x)
            )
        slot = 1 + way if step == 1 else 3
        send(block, block, cx_s.at[slot, c], cx_r.at[slot, c], at(y, z, core + 1), x)

    def gradient(order, slot):
        zo = zs[order]
        into = grad if slot is None else gsum.at[slot]

        def pick(n, carry):
            chosen[pl.ds(pl.multiple_of(n * BAGS, BAGS), BAGS), :] = cot_all[n, tile_nums[n, order, 0]]
            return carry

        lax.fori_loop(0, PLANE, pick, 0)

        def block(b, carry):
            rows = pl.ds(pl.multiple_of(b * DIM, DIM), DIM)
            into[rows, :] = jnp.dot(counts[zo, rows, :], chosen[...], preferred_element_type=jnp.float32)
            return carry

        lax.fori_loop(0, ROWS // DIM, block, 0)

    def pass_grad(way, dist, block, slot):
        rows = slice(block * DIM, (block + 1) * DIM)
        add = dist < 3 or (dist == 3 and (block < 2) == (way == 0))
        held = gfar.at[way] if dist == 4 else grecv.at[way, dist]
        value = gsum[slot, rows, :]
        if add:
            arrived(held.at[rows], g_r.at[way, dist, block])
            value = value + held[rows, :].astype(jnp.float32)
        room(grad_stream[way], 3)
        spot_rows = rows if dist < 4 else slice(block % 2 * DIM, (block % 2 + 1) * DIM)
        held[spot_rows, :] = value.astype(jnp.bfloat16)
        target = plane(z + 1) if way == 0 else plane(z - 1)
        grad_stream[way].append(
            send(
                held.at[spot_rows], grecv.at[way, dist - 1, rows],
                g_s.at[way, dist - 1, block], g_r.at[way, dist - 1, block], at(y, target, core), x,
            )
        )

    early, late = ((2, 3), (0, 1)), ((0, 1), (2, 3))
    grad_steps = [(dist, blocks, k) for dist, blocks in (
        (4, late), (3, early), (3, late), (2, early), (2, late), (1, early), (1, late)
    ) for k in (0, 1)]

    def grads_step(i):
        dist, blocks, k = grad_steps[i]
        for way in (0, 1):
            pass_grad(way, dist, blocks[way][k], way if dist < 4 else 0)

    zs = [z] + [plane(z - s) if w == 0 else plane(z + s) for s in (1, 2, 3) for w in (0, 1)] + [plane(z + 4)]

    def build_next(order):
        arrived(idx.at[zs[order]], ix_r.at[(order + 1) // 2 if order % 2 else NZ - (order + 1) // 2])
        build(zs[order], order)

    def move_acc():
        acc_in.wait()
        acc_half[...] = acc_full[...].astype(jnp.bfloat16)
        for j in range(1, NX):
            owner = lax.rem(x + j, NX)
            send(
                acc_half.at[:, lanes(owner * ROWS, ROWS)], acc_own.at[feature_rows(x)],
                ax_s.at[j - 1], ax_r.at[j - 1], t, owner,
            )
        acc_own[feature_rows(x), :] = acc_half[:, lanes(x * ROWS, ROWS)]

    rows_step(1)
    send_cot(1)
    for c in range(4):
        send(cot_ref.at[tiles4(c)], cot_all.at[me, tiles4(c)], cx_s.at[0, c], cx_r.at[0, c], at(y, z, core + 1), x)
    build(z, 0)
    rows_step(2)
    move_acc()
    rows_step(3)
    send_cot(2)
    build_next(1)
    rows_step(4)
    pool(zs[0])
    rows_step(5)
    send_cot(3)
    build_next(2)
    rows_step(6)
    build_next(3)
    rows_step(7)
    relay_cot(0, 1, 0)
    relay_cot(1, 1, 2)
    build_next(4)
    rows_step(8)
    relay_cot(0, 1, 2)
    relay_cot(1, 1, 0)
    pool(zs[1])
    rows_step(9)
    relay_cot(0, 1, 1)
    relay_cot(1, 1, 3)
    pool(zs[2])
    rows_step(10)
    relay_cot(0, 1, 3)
    relay_cot(1, 1, 1)
    build_next(7)
    rows_step(11)
    build_next(5)
    relay_cot(0, 2, 0)
    relay_cot(1, 2, 2)
    build_next(6)
    pool(zs[3])

    to_scalars = local(tile_rows, tile_nums, 9)
    for k, (dy, dc) in enumerate(others):
        dest = spot(y + dy, core + dc)
        send(tile_rows.at[dest], tiles.at[me], t_s.at[k], t_r.at[k], at(y + dy, z, core + dc), x)
    tiles[me] = tile_rows[me]
    relay_cot(0, 2, 1)
    relay_cot(1, 2, 3)
    for order in (0, 1, 2, 3):
        send_part(order)
    to_scalars.wait()
    own_cot.wait()
    for c in range(4):
        arrived(cot_all.at[spot(y, core + 1), tiles4(c)], cx_r.at[0, c])
        arrived(cot_all.at[spot(y - 1, core + 1), tiles4(c)], cx_r.at[1, c])
        arrived(cot_all.at[spot(y + 1, core + 1), tiles4(c)], cx_r.at[2, c])
        arrived(cot_all.at[spot(y + 2, core + 1), tiles4(c)], cx_r.at[3, c])

    gradient(7, 0)
    grads_step(0)
    rows_step(12)
    gradient(5, 1)
    grads_step(1)
    rows_step(13)
    gradient(6, 0)
    grads_step(2)
    pool(zs[4])
    grads_step(3)
    send_part(4)
    for k in (0, 1):
        wait_rows(0, 3, k + 2, lax.rem(x - ORDER[k + 2] + NX, NX))
        wait_rows(1, 3, k, lax.rem(x - ORDER[k] + NX, NX))
    pool(zs[5])
    grads_step(4)
    pool(zs[6])
    grads_step(5)
    send_part(5)
    gradient(4, 0)
    gradient(3, 1)
    grads_step(6)
    send_part(6)

    for k, (dy, dc) in enumerate(others):
        arrived(tiles.at[spot(y - dy, core - dc)], t_r.at[k])
    held = tiles[...].reshape(PAIRS, BAGS)
    down = lax.broadcasted_iota(jnp.int32, (PAIRS, BAGS), 0)
    across = lax.broadcasted_iota(jnp.int32, (PAIRS, BAGS), 1)
    tile_line = jnp.sum(jnp.where(down == across, held, 0), axis=0, keepdims=True)
    turn_down = ((down & 7) << 3) + (down >> 3)
    turn_across = ((across & 7) << 3) + (across >> 3)

    def last_of(found, turn):
        last = jnp.max(jnp.where(found, turn, -1), axis=1, keepdims=True)
        return jnp.broadcast_to(jnp.where(last < 0, PAIRS, last), (last.shape[0], BAGS))

    codes[:PAIRS] = last_of((tile_line == held) & (turn_across < turn_down) & (across < PAIRS), turn_across)
    codes[PAIRS:] = last_of((tile_line == down[:TILES]) & (across[:TILES] < PAIRS), turn_across[:TILES])
    to_codes = local(codes, code_nums, 16)
    sums[PAIRS] = jnp.zeros((DIM, BAGS), jnp.float32)

    grads_step(7)
    for k in range(NX):
        wait_rows(0 if k < 2 else 1, 4, k, lax.rem(x - ORDER[k] + NX, NX))
    pool(zs[7])
    grads_step(8)
    send_part(7)
    grads_step(9)
    gradient(2, 0)
    gradient(1, 1)
    grads_step(10)

    for j in range(1, NX):
        arrived(acc_own.at[feature_rows(lax.rem(x - j + NX, NX))], ax_r.at[j - 1])

    def turn(b, carry):
        rows = pl.ds(pl.multiple_of(b * 128, 128), 128)
        own[rows, :] = emb_all[z, :, rows].astype(jnp.float32).T.astype(jnp.bfloat16)
        state[rows, :] = acc_own[:, rows].astype(jnp.float32).T.astype(jnp.bfloat16)
        return carry

    lax.fori_loop(0, ROWS // 128, turn, 0)
    grads_step(11)
    to_codes.wait()

    def fold(order):
        for k, (dy, dc) in enumerate(others):
            arrived(arr.at[spot(y - dy, core - dc), order], p_r.at[order, k])

        def one(n, carry):
            sums[order * PLANE + n] = arr[n, order].astype(jnp.float32) + sums[code_nums[n * NZ + order, 0]]
            return carry

        lax.fori_loop(0, PLANE, one, 0)

    gradient(0, None)
    fold(0)
    fold(1)
    grads_step(12)
    fold(2)
    grads_step(13)
    for order in range(3, NZ):
        fold(order)
    outs = []

    def pool_out(k, carry):
        pooled[k] = sums[code_nums[PAIRS + k, 0]].T.astype(jnp.bfloat16)
        return carry

    for quarter in range(4):
        lax.fori_loop(4 * quarter, 4 * quarter + 4, pool_out, 0)
        outs.append(local(pooled.at[tiles4(quarter)], pooled_ref.at[tiles4(quarter)], 25 + quarter))
    for block in (0, 2, 1, 3):
        rows = slice(block * DIM, (block + 1) * DIM)
        for way in (0, 1):
            arrived(grecv.at[way, 0, rows], g_r.at[way, 0, block])
        got = grad[rows, :] + grecv[0, 0, rows, :].astype(jnp.float32) + grecv[1, 0, rows, :].astype(jnp.float32)
        new_state = state[rows, :].astype(jnp.float32) + got * got
        grad[rows, :] = new_state
        own[rows, :] = (
            own[rows, :].astype(jnp.float32) - LEARN_RATE * got / (jnp.sqrt(new_state) + EPSILON)
        ).astype(jnp.bfloat16)
        outs.append(local(grad.at[rows], new_sums_ref.at[rows], 17 + block))
        outs.append(local(own.at[rows], new_rows_ref.at[rows], 21 + block))
    for copy in outs:
        copy.wait()
    for copy in sent:
        copy.wait_send()


def hand_over_kernel(pooled_in, rows_in, sums_in, pooled_ref, rows_ref, sums_ref, pooled, rows, sums, sem_in, sem_out):
    pieces = []
    for source, held, target, count in (
        (pooled_in, pooled, pooled_ref, 4), (sums_in, sums, sums_ref, 4), (rows_in, rows, rows_ref, 2)
    ):
        size = source.shape[0] // count
        for k in range(count):
            part, n = pl.ds(k * size, size), len(pieces)
            pieces.append((
                pltpu.make_async_copy(source.at[part], held.at[part], sem_in.at[n]),
                pltpu.make_async_copy(held.at[part], target.at[part], sem_out.at[n]),
            ))
    for load, _ in pieces:
        load.start()
    for load, store in pieces:
        load.wait()
        store.start()
    for _, store in pieces:
        store.wait()


def per_device(embedding, accumulator, pair_rows, pair_len, pair_dest, pair_tile, pooled_grad):
    hbm = pl.BlockSpec(memory_space=pl.ANY)
    bf16, f32, i32 = jnp.bfloat16, jnp.float32, jnp.int32
    dma = pltpu.SemaphoreType.DMA
    sems = [(3,), (3,), (3,), (3,), (8,), (8,), (2, 5, 4), (2, 5, 4), (2, 3, 4), (2, 3, 4), (4, 4), (4, 4),
            (8, 7), (8, 7), (7,), (7,), (2, 4, 4), (2, 4, 4), (29,)]
    pooled, new_rows, new_state = pl.pallas_call(
        move_kernel,
        out_shape=(
            jax.ShapeDtypeStruct((TILES, BAGS, DIM), bf16),
            jax.ShapeDtypeStruct((ROWS, DIM), bf16),
            jax.ShapeDtypeStruct((ROWS, DIM), f32),
        ),
        in_specs=[hbm] * 7,
        out_specs=[hbm] * 3,
        scratch_shapes=[
            pltpu.VMEM((NZ, DIM, ROWS), bf16),
            pltpu.VMEM((NZ, ROWS, SPAN), bf16),
            pltpu.VMEM((PLANE, TILES, BAGS, DIM), bf16),
            pltpu.VMEM((NZ, PLANE, DIM, BAGS), bf16),
            pltpu.VMEM((PLANE, NZ, BAGS), i32),
            pltpu.VMEM((NZ, LOOK, PLANE, BAGS), i32),
            pltpu.VMEM((NZ, LOOK, PLANE, BAGS), i32),
            pltpu.VMEM((2, ROWS // 2, DIM), bf16),
            pltpu.VMEM((2, 4, ROWS, DIM), bf16),
            pltpu.VMEM((2, ROWS, DIM), f32),
            pltpu.VMEM((SPAN, DIM), bf16),
            pltpu.VMEM((FEAT, NX * ROWS), bf16),
            pltpu.VMEM((DIM, ROWS), bf16),
            pltpu.VMEM((DIM, BAGS), bf16),
            pltpu.SMEM((PLANE, NZ, BAGS), i32),
            pltpu.VMEM((FEAT, NX * ROWS), f32),
            pltpu.VMEM((PAIRS, BAGS), i32),
            pltpu.VMEM((PAIRS, LOOK, BAGS), i32),
            pltpu.VMEM((1, PAIRS), i32),
            pltpu.VMEM((1, PAIRS), i32),
            pltpu.VMEM((PLANE, NZ, DIM, BAGS), bf16),
            pltpu.VMEM((PLANE, NZ, BAGS), i32),
            pltpu.VMEM((PAIRS + 1, DIM, BAGS), f32),
            pltpu.VMEM((PAIRS + TILES, BAGS), i32),
            pltpu.SMEM((PAIRS + TILES, BAGS), i32),
            pltpu.VMEM((TILES, BAGS, DIM), bf16),
            pltpu.VMEM((ROWS, DIM), f32),
            pltpu.VMEM((ROWS, DIM), bf16),
            pltpu.VMEM((ROWS, DIM), bf16),
        ]
        + [dma(s) for s in sems],
        compiler_params=pltpu.CompilerParams(collective_id=0, has_side_effects=True, vmem_limit_bytes=60 << 20),
        name="move_rows_and_tiles",
    )(
        embedding.T, accumulator.T, pooled_grad.reshape(TILES, BAGS, DIM),
        pair_len, jnp.transpose(pair_rows, (0, 2, 1)), pair_dest, pair_tile,
    )
    pooled, new_rows, new_state = pl.pallas_call(
        hand_over_kernel,
        out_shape=(
            jax.ShapeDtypeStruct((TILES, BAGS, DIM), bf16),
            jax.ShapeDtypeStruct((ROWS, DIM), bf16),
            jax.ShapeDtypeStruct((ROWS, DIM), f32),
        ),
        in_specs=[hbm] * 3,
        out_specs=[hbm] * 3,
        scratch_shapes=[
            pltpu.VMEM((TILES, BAGS, DIM), bf16),
            pltpu.VMEM((ROWS, DIM), bf16),
            pltpu.VMEM((ROWS, DIM), f32),
            dma((10,)),
            dma((10,)),
        ],
        compiler_params=pltpu.CompilerParams(vmem_limit_bytes=60 << 20),
        name="hand_over",
    )(pooled, new_rows, new_state)
    return (pooled.reshape(TILES * BAGS, DIM), new_rows, new_state)


def solution(mesh):
    return jax.shard_map(
        per_device,
        mesh=mesh,
        in_specs=(
            P("table", "col"),
            P("table", "col"),
            P(("table", "col"), None, None),
            P(("table", "col"), None),
            P(("table", "col"), None),
            P(("table", "col"), None),
            P(("table", "col"), None),
        ),
        out_specs=(P(("table", "col"), None), P(("table", "col"), None), P(("table", "col"), None)),
        check_vma=False,
    )
```

```python
import functools
import jax
import jax.numpy as jnp
from jax import lax
from jax.experimental import pallas as pl
from jax.experimental.pallas import tpu as pltpu
from jax.sharding import PartitionSpec as P

LEARN_RATE = 0.3
EPSILON = 1e-08
MESH = pl.DeviceIdType.MESH
NY, NZ, NCORE, NX = 4, 8, 2, 4
PLANE = NY * NCORE
ROWS = 1024
DIM = 256
BAGS = 128
LOOK = 4
TILES = 16
FEAT = DIM // NX
SPAN = PLANE * BAGS
TILE_UNIT = 2048
PAIRS = NZ * PLANE
HALF = DIM // 2


def move_kernel(
    emb_ref, acc_ref, cot_ref, lens_ref, rows_ref, dest_ref, tile_ref,
    pooled_ref, new_rows_ref, new_sums_ref,
    emb_all, counts, cot_all, part, tile_rows, idx, msg, gfar, grecv, gsum, chosen, acc_half, acc_own, row_ids, tile_nums,
    acc_full, lens, pair_rows, dests, pair_tiles, arr, tiles, sums, codes, code_nums, pooled, grad, own, state,
    ex_s, ex_r, ax_s, ax_r, ix_s, ix_r, e_s, e_r, cy_s, cy_r, cx_s, cx_r, p_s, p_r, t_s, t_r, g_s, g_r, loc,
):
    t = lax.axis_index("table")
    x = lax.axis_index("col")
    y, z, core = t // (NZ * NCORE), (t // NCORE) % NZ, t % NCORE

    def at(yy, zz, cc):
        return (lax.rem(yy + NY, NY) * NZ + lax.rem(zz + NZ, NZ)) * NCORE + lax.rem(cc + NCORE, NCORE)

    def plane(zz):
        return lax.rem(zz + 2 * NZ, NZ)

    def spot(yy, cc):
        return lax.rem(yy + NY, NY) * NCORE + lax.rem(cc + NCORE, NCORE)

    me = spot(y, core)
    others = [(dy, dc) for dy in (2, 1, 3, 0) for dc in (0, 1) if (dy, dc) != (0, 0)]

    barrier = pltpu.get_barrier_semaphore()
    for j in range(1, NX):
        pl.semaphore_signal(barrier, inc=1, device_id=(t, lax.rem(x + j, NX)), device_id_type=MESH)
    for j in range(1, NZ):
        pl.semaphore_signal(barrier, inc=1, device_id=(at(y, z + j, core), x), device_id_type=MESH)
    for dy, dc in others:
        pl.semaphore_signal(barrier, inc=1, device_id=(at(y + dy, z, core + dc), x), device_id_type=MESH)

    def local(src, dst, k):
        copy = pltpu.make_async_copy(src, dst, loc.at[k])
        copy.start()
        return copy

    def feature_rows(q):
        return pl.ds(pl.multiple_of(q * FEAT, FEAT), FEAT)

    def lanes(start, size):
        return pl.ds(pl.multiple_of(start, 128), size)

    small = [
        local(rows_ref, pair_rows, 10), local(lens_ref, lens, 11),
        local(dest_ref, dests, 12), local(tile_ref, pair_tiles, 13),
    ]
    own_rows = local(emb_ref.at[:, lanes(x * ROWS, ROWS)], emb_all.at[z, feature_rows(x)], 14)
    acc_in = local(acc_ref, acc_full, 15)
    own_cot = local(cot_ref, cot_all.at[me], 0)
    pl.semaphore_wait(barrier, NX - 1 + NZ - 1 + PLANE - 1)

    sent = []

    def send(src, dst, send_sem, recv_sem, table, col):
        copy = pltpu.make_async_remote_copy(
            src_ref=src, dst_ref=dst, send_sem=send_sem, recv_sem=recv_sem, device_id=(table, col), device_id_type=MESH
        )
        copy.start()
        sent.append(copy)
        return copy

    def room(stream, most):
        if len(stream) == most:
            first = stream.pop(0)
            first.wait_send()
            sent[:] = [copy for copy in sent if copy is not first]

    def arrived(dst, recv_sem):
        pltpu.make_async_copy(dst, dst, recv_sem).wait()

    for j in (1, 3, 2):
        owner = lax.rem(x + j, NX)
        send(
            emb_ref.at[:, lanes(owner * ROWS, ROWS)], emb_all.at[z, feature_rows(x)],
            ex_s.at[j - 1], ex_r.at[j - 1], t, owner,
        )

    ORDER = (0, 1, 3, 2)

    def pass_rows(way, step, order, q):
        source = plane(z - step) if way == 0 else plane(z + step)
        target = plane(z + 1) if way == 0 else plane(z - 1)
        block = emb_all.at[source, feature_rows(q)]
        return send(block, block, e_s.at[way, step, order], e_r.at[way, step + 1, order], at(y, target, core), x)

    def wait_rows(way, step, order, q):
        source = plane(z - step) if way == 0 else plane(z + step)
        arrived(emb_all.at[source, feature_rows(q)], e_r.at[way, step, order])

    row_stream, cot_stream, grad_stream = ([], []), ([], []), ([], [])

    def rows_step(i):
        step, k = i // NX, i % NX
        if i == 0:
            own_rows.wait()
        elif step == 0:
            arrived(emb_all.at[z, feature_rows(lax.rem(x - ORDER[k] + NX, NX))], ex_r.at[ORDER[k] - 1])
        for way in (0, 1):
            kk = k + 2 * way if step == 3 else k
            q = lax.rem(x - ORDER[kk] + NX, NX)
            if step:
                wait_rows(way, step, kk, q)
            room(row_stream[way], 3)
            row_stream[way].append(pass_rows(way, step, kk, q))

    rows_step(0)

    def tiles4(c):
        return pl.ds(4 * c, 4)

    def send_cot(c):
        for way, dy in ((0, 1), (1, -1)):
            c_way = c if way == 0 else (c + 2) % 4
            room(cot_stream[way], 2)
            cot_stream[way].append(
                send(
                    cot_ref.at[tiles4(c_way)], cot_all.at[me, tiles4(c_way)],
                    cy_s.at[way, 0, c_way], cy_r.at[way, 1, c_way], at(y + dy, z, core), x,
                )
            )

    send_cot(0)

    for copy in small:
        copy.wait()
    place = lax.broadcasted_iota(jnp.int32, (PAIRS, PAIRS), 0)
    where_to = ((place & 7) >> 1) * (NZ * NCORE) + (place >> 3) * NCORE + (place & 1)
    match = dests[...] == where_to
    pick_pair = jnp.where(match, 1.0, 0.0).astype(jnp.bfloat16)
    pair_tile = jnp.sum(jnp.where(match, pair_tiles[...], 0), axis=1, keepdims=True)
    for l in range(LOOK):
        row = jnp.where(lens[...] > l, pair_rows[:, l, :], ROWS)
        high = (row >> 5).astype(jnp.float32).astype(jnp.bfloat16)
        low = (row & 31).astype(jnp.float32).astype(jnp.bfloat16)
        got = jnp.dot(pick_pair, high, preferred_element_type=jnp.float32) * 32.0 + jnp.dot(
            pick_pair, low, preferred_element_type=jnp.float32
        )
        msg[:, l] = (got.astype(jnp.int32) + pair_tile * TILE_UNIT).reshape(NZ, PLANE, BAGS)
    for off in (1, 7, 2, 6, 3, 5, 4):
        target = plane(z + off)
        send(msg.at[target], idx.at[z], ix_s.at[off], ix_r.at[off], at(y, target, core), x)
    idx[z] = msg[z]

    ids = lax.broadcasted_iota(jnp.int32, (DIM, BAGS), 0)
    row_ids[...] = ids.astype(jnp.float32).astype(jnp.bfloat16)

    def build(zo, order):
        one, zero = jnp.ones((), jnp.bfloat16), jnp.zeros((), jnp.bfloat16)

        def pair(n, carry):
            held = [idx[zo, l, pl.ds(n, 1), :] for l in range(LOOK)]
            tile_rows[n, order : order + 1, :] = (held[0] >> 11) & (TILES - 1)
            for block in range(ROWS // DIM):
                total = None
                for l in range(LOOK):
                    near = jnp.clip((held[l] & (TILE_UNIT - 1)) - block * DIM, -1, DIM)
                    hit = jnp.where(row_ids[...] == near.astype(jnp.float32).astype(jnp.bfloat16), one, zero)
                    total = hit if total is None else total + hit
                counts[zo, pl.ds(block * DIM, DIM), lanes(n * BAGS, BAGS)] = total
            return carry

        lax.fori_loop(0, PLANE, pair, 0)

    def pool(zo):
        def block(b, carry):
            got = jnp.dot(
                emb_all[zo], counts[zo, :, lanes(b * DIM, DIM)], preferred_element_type=jnp.float32
            ).astype(jnp.bfloat16)
            part[zo, 2 * b] = got[:, :BAGS]
            part[zo, 2 * b + 1] = got[:, BAGS:]
            return carry

        lax.fori_loop(0, SPAN // DIM, block, 0)

    def send_part(order):
        zo = zs[order]
        for k, (dy, dc) in enumerate(others):
            dest = spot(y + dy, core + dc)
            send(part.at[zo, dest], arr.at[me, order], p_s.at[order, k], p_r.at[order, k], at(y + dy, z, core + dc), x)
        arr[me, order] = part[zo, me]

    def relay_cot(way, step, c):
        dy = 1 if way == 0 else -1
        source = spot(y - dy * step, core)
        block = cot_all.at[source, tiles4(c)]
        arrived(block, cy_r.at[way, step, c])
        if step == 1 and c // 2 == way:
            room(cot_stream[way], 2)
            cot_stream[way].append(
                send(block, block, cy_s.at[way, 1, c], cy_r.at[way, 2, c], at(y + dy, z, core), x)
            )
        slot = 1 + way if step == 1 else 3
        send(block, block, cx_s.at[slot, c], cx_r.at[slot, c], at(y, z, core + 1), x)

    def gradient(order, slot):
        zo = zs[order]
        into = grad if slot is None else gsum.at[slot]

        def pick(n, carry):
            chosen[pl.ds(pl.multiple_of(n * BAGS, BAGS), BAGS), :] = cot_all[n, tile_nums[n, order, 0]]
            return carry

        lax.fori_loop(0, PLANE, pick, 0)

        def block(b, carry):
            rows = pl.ds(pl.multiple_of(b * DIM, DIM), DIM)
            into[rows, :] = jnp.dot(counts[zo, rows, :], chosen[...], preferred_element_type=jnp.float32)
            return carry

        lax.fori_loop(0, ROWS // DIM, block, 0)

    def pass_grad(way, dist, block, slot):
        rows = slice(block * DIM, (block + 1) * DIM)
        add = dist < 3 or (dist == 3 and (block < 2) == (way == 0))
        held = gfar.at[way] if dist == 4 else grecv.at[way, dist]
        value = gsum[slot, rows, :]
        if add:
            arrived(held.at[rows], g_r.at[way, dist, block])
            value = value + held[rows, :].astype(jnp.float32)
        room(grad_stream[way], 3)
        spot_rows = rows if dist < 4 else slice(block % 2 * DIM, (block % 2 + 1) * DIM)
        held[spot_rows, :] = value.astype(jnp.bfloat16)
        target = plane(z + 1) if way == 0 else plane(z - 1)
        grad_stream[way].append(
            send(
                held.at[spot_rows], grecv.at[way, dist - 1, rows],
                g_s.at[way, dist - 1, block], g_r.at[way, dist - 1, block], at(y, target, core), x,
            )
        )

    early, late = ((2, 3), (0, 1)), ((0, 1), (2, 3))
    grad_steps = [(dist, blocks, k) for dist, blocks in (
        (4, late), (3, early), (3, late), (2, early), (2, late), (1, early), (1, late)
    ) for k in (0, 1)]

    def grads_step(i):
        dist, blocks, k = grad_steps[i]
        for way in (0, 1):
            pass_grad(way, dist, blocks[way][k], way if dist < 4 else 0)

    zs = [z] + [plane(z - s) if w == 0 else plane(z + s) for s in (1, 2, 3) for w in (0, 1)] + [plane(z + 4)]

    def build_next(order):
        arrived(idx.at[zs[order]], ix_r.at[(order + 1) // 2 if order % 2 else NZ - (order + 1) // 2])
        build(zs[order], order)

    def move_acc():
        acc_in.wait()
        acc_half[...] = acc_full[...].astype(jnp.bfloat16)
        for j in range(1, NX):
            owner = lax.rem(x + j, NX)
            send(
                acc_half.at[:, lanes(owner * ROWS, ROWS)], acc_own.at[feature_rows(x)],
                ax_s.at[j - 1], ax_r.at[j - 1], t, owner,
            )
        acc_own[feature_rows(x), :] = acc_half[:, lanes(x * ROWS, ROWS)]

    rows_step(1)
    send_cot(1)
    for c in range(4):
        send(cot_ref.at[tiles4(c)], cot_all.at[me, tiles4(c)], cx_s.at[0, c], cx_r.at[0, c], at(y, z, core + 1), x)
    build(z, 0)
    rows_step(2)
    move_acc()
    rows_step(3)
    send_cot(2)
    build_next(1)
    rows_step(4)
    pool(zs[0])
    rows_step(5)
    send_cot(3)
    build_next(2)
    rows_step(6)
    build_next(3)
    rows_step(7)
    relay_cot(0, 1, 0)
    relay_cot(1, 1, 2)
    build_next(4)
    rows_step(8)
    relay_cot(0, 1, 2)
    relay_cot(1, 1, 0)
    pool(zs[1])
    rows_step(9)
    relay_cot(0, 1, 1)
    relay_cot(1, 1, 3)
    pool(zs[2])
    rows_step(10)
    relay_cot(0, 1, 3)
    relay_cot(1, 1, 1)

    for j in range(1, NX):
        arrived(acc_own.at[feature_rows(lax.rem(x - j + NX, NX))], ax_r.at[j - 1])

    def turn(b, carry):
        rows = pl.ds(pl.multiple_of(b * 128, 128), 128)
        own[rows, :] = emb_all[z, :, rows].astype(jnp.float32).T.astype(jnp.bfloat16)
        state[rows, :] = acc_own[:, rows].astype(jnp.float32).T.astype(jnp.bfloat16)
        return carry

    lax.fori_loop(0, ROWS // 128, turn, 0)
    build_next(7)
    rows_step(11)
    build_next(5)
    relay_cot(0, 2, 0)
    relay_cot(1, 2, 2)
    build_next(6)
    pool(zs[3])

    to_scalars = local(tile_rows, tile_nums, 9)
    for k, (dy, dc) in enumerate(others):
        dest = spot(y + dy, core + dc)
        send(tile_rows.at[dest], tiles.at[me], t_s.at[k], t_r.at[k], at(y + dy, z, core + dc), x)
    tiles[me] = tile_rows[me]
    relay_cot(0, 2, 1)
    relay_cot(1, 2, 3)
    for order in (0, 1, 2, 3):
        send_part(order)
    to_scalars.wait()
    own_cot.wait()
    for c in range(4):
        arrived(cot_all.at[spot(y, core + 1), tiles4(c)], cx_r.at[0, c])
        arrived(cot_all.at[spot(y - 1, core + 1), tiles4(c)], cx_r.at[1, c])
        arrived(cot_all.at[spot(y + 1, core + 1), tiles4(c)], cx_r.at[2, c])
        arrived(cot_all.at[spot(y + 2, core + 1), tiles4(c)], cx_r.at[3, c])

    gradient(7, 0)
    grads_step(0)
    rows_step(12)
    gradient(5, 1)
    grads_step(1)
    rows_step(13)
    gradient(6, 0)
    grads_step(2)
    pool(zs[4])
    grads_step(3)
    send_part(4)
    for k in (0, 1):
        wait_rows(0, 3, k + 2, lax.rem(x - ORDER[k + 2] + NX, NX))
        wait_rows(1, 3, k, lax.rem(x - ORDER[k] + NX, NX))
    pool(zs[5])
    grads_step(4)
    pool(zs[6])
    grads_step(5)
    send_part(5)
    gradient(4, 0)
    gradient(3, 1)
    grads_step(6)
    send_part(6)

    for k, (dy, dc) in enumerate(others):
        arrived(tiles.at[spot(y - dy, core - dc)], t_r.at[k])
    held = tiles[...].reshape(PAIRS, BAGS)
    down = lax.broadcasted_iota(jnp.int32, (PAIRS, BAGS), 0)
    across = lax.broadcasted_iota(jnp.int32, (PAIRS, BAGS), 1)
    tile_line = jnp.sum(jnp.where(down == across, held, 0), axis=0, keepdims=True)
    turn_down = ((down & 7) << 3) + (down >> 3)
    turn_across = ((across & 7) << 3) + (across >> 3)

    def last_of(found, turn):
        last = jnp.max(jnp.where(found, turn, -1), axis=1, keepdims=True)
        return jnp.broadcast_to(jnp.where(last < 0, PAIRS, last), (last.shape[0], BAGS))

    codes[:PAIRS] = last_of((tile_line == held) & (turn_across < turn_down) & (across < PAIRS), turn_across)
    codes[PAIRS:] = last_of((tile_line == down[:TILES]) & (across[:TILES] < PAIRS), turn_across[:TILES])
    to_codes = local(codes, code_nums, 16)
    sums[PAIRS] = jnp.zeros((DIM, BAGS), jnp.float32)

    grads_step(7)
    for k in range(NX):
        wait_rows(0 if k < 2 else 1, 4, k, lax.rem(x - ORDER[k] + NX, NX))
    pool(zs[7])
    grads_step(8)
    send_part(7)
    grads_step(9)
    gradient(2, 0)
    gradient(1, 1)
    grads_step(10)

    grads_step(11)
    to_codes.wait()

    def fold(order):
        for k, (dy, dc) in enumerate(others):
            arrived(arr.at[spot(y - dy, core - dc), order], p_r.at[order, k])

        def one(n, carry):
            sums[order * PLANE + n] = arr[n, order].astype(jnp.float32) + sums[code_nums[n * NZ + order, 0]]
            return carry

        lax.fori_loop(0, PLANE, one, 0)

    fold(0)
    fold(1)
    grads_step(12)
    fold(2)
    grads_step(13)
    gradient(0, None)
    for order in range(3, NZ):
        fold(order)
    outs = []

    def pool_out(k, carry):
        pooled[k] = sums[code_nums[PAIRS + k, 0]].T.astype(jnp.bfloat16)
        return carry

    for quarter in range(4):
        lax.fori_loop(4 * quarter, 4 * quarter + 4, pool_out, 0)
        outs.append(local(pooled.at[tiles4(quarter)], pooled_ref.at[tiles4(quarter)], 25 + quarter))
    for block in (0, 2, 1, 3):
        rows = slice(block * DIM, (block + 1) * DIM)
        for way in (0, 1):
            arrived(grecv.at[way, 0, rows], g_r.at[way, 0, block])
        got = grad[rows, :] + grecv[0, 0, rows, :].astype(jnp.float32) + grecv[1, 0, rows, :].astype(jnp.float32)
        new_state = state[rows, :].astype(jnp.float32) + got * got
        grad[rows, :] = new_state
        own[rows, :] = (
            own[rows, :].astype(jnp.float32) - LEARN_RATE * got / (jnp.sqrt(new_state) + EPSILON)
        ).astype(jnp.bfloat16)
        outs.append(local(grad.at[rows], new_sums_ref.at[rows], 17 + block))
        outs.append(local(own.at[rows], new_rows_ref.at[rows], 21 + block))
    for copy in outs:
        copy.wait()
    for copy in sent:
        copy.wait_send()


def hand_over_kernel(pooled_in, rows_in, sums_in, pooled_ref, rows_ref, sums_ref, pooled, rows, sums, sem_in, sem_out):
    pieces = []
    for source, held, target, count in (
        (pooled_in, pooled, pooled_ref, 4), (sums_in, sums, sums_ref, 4), (rows_in, rows, rows_ref, 2)
    ):
        size = source.shape[0] // count
        for k in range(count):
            part, n = pl.ds(k * size, size), len(pieces)
            pieces.append((
                pltpu.make_async_copy(source.at[part], held.at[part], sem_in.at[n]),
                pltpu.make_async_copy(held.at[part], target.at[part], sem_out.at[n]),
            ))
    for load, _ in pieces:
        load.start()
    for load, store in pieces:
        load.wait()
        store.start()
    for _, store in pieces:
        store.wait()


def per_device(embedding, accumulator, pair_rows, pair_len, pair_dest, pair_tile, pooled_grad):
    hbm = pl.BlockSpec(memory_space=pl.ANY)
    bf16, f32, i32 = jnp.bfloat16, jnp.float32, jnp.int32
    dma = pltpu.SemaphoreType.DMA
    sems = [(3,), (3,), (3,), (3,), (8,), (8,), (2, 5, 4), (2, 5, 4), (2, 3, 4), (2, 3, 4), (4, 4), (4, 4),
            (8, 7), (8, 7), (7,), (7,), (2, 4, 4), (2, 4, 4), (29,)]
    pooled, new_rows, new_state = pl.pallas_call(
        move_kernel,
        out_shape=(
            jax.ShapeDtypeStruct((TILES, BAGS, DIM), bf16),
            jax.ShapeDtypeStruct((ROWS, DIM), bf16),
            jax.ShapeDtypeStruct((ROWS, DIM), f32),
        ),
        in_specs=[hbm] * 7,
        out_specs=[hbm] * 3,
        scratch_shapes=[
            pltpu.VMEM((NZ, DIM, ROWS), bf16),
            pltpu.VMEM((NZ, ROWS, SPAN), bf16),
            pltpu.VMEM((PLANE, TILES, BAGS, DIM), bf16),
            pltpu.VMEM((NZ, PLANE, DIM, BAGS), bf16),
            pltpu.VMEM((PLANE, NZ, BAGS), i32),
            pltpu.VMEM((NZ, LOOK, PLANE, BAGS), i32),
            pltpu.VMEM((NZ, LOOK, PLANE, BAGS), i32),
            pltpu.VMEM((2, ROWS // 2, DIM), bf16),
            pltpu.VMEM((2, 4, ROWS, DIM), bf16),
            pltpu.VMEM((2, ROWS, DIM), f32),
            pltpu.VMEM((SPAN, DIM), bf16),
            pltpu.VMEM((FEAT, NX * ROWS), bf16),
            pltpu.VMEM((DIM, ROWS), bf16),
            pltpu.VMEM((DIM, BAGS), bf16),
            pltpu.SMEM((PLANE, NZ, BAGS), i32),
            pltpu.VMEM((FEAT, NX * ROWS), f32),
            pltpu.VMEM((PAIRS, BAGS), i32),
            pltpu.VMEM((PAIRS, LOOK, BAGS), i32),
            pltpu.VMEM((1, PAIRS), i32),
            pltpu.VMEM((1, PAIRS), i32),
            pltpu.VMEM((PLANE, NZ, DIM, BAGS), bf16),
            pltpu.VMEM((PLANE, NZ, BAGS), i32),
            pltpu.VMEM((PAIRS + 1, DIM, BAGS), f32),
            pltpu.VMEM((PAIRS + TILES, BAGS), i32),
            pltpu.SMEM((PAIRS + TILES, BAGS), i32),
            pltpu.VMEM((TILES, BAGS, DIM), bf16),
            pltpu.VMEM((ROWS, DIM), f32),
            pltpu.VMEM((ROWS, DIM), bf16),
            pltpu.VMEM((ROWS, DIM), bf16),
        ]
        + [dma(s) for s in sems],
        compiler_params=pltpu.CompilerParams(collective_id=0, has_side_effects=True, vmem_limit_bytes=60 << 20),
        name="move_rows_and_tiles",
    )(
        embedding.T, accumulator.T, pooled_grad.reshape(TILES, BAGS, DIM),
        pair_len, jnp.transpose(pair_rows, (0, 2, 1)), pair_dest, pair_tile,
    )
    pooled, new_rows, new_state = pl.pallas_call(
        hand_over_kernel,
        out_shape=(
            jax.ShapeDtypeStruct((TILES, BAGS, DIM), bf16),
            jax.ShapeDtypeStruct((ROWS, DIM), bf16),
            jax.ShapeDtypeStruct((ROWS, DIM), f32),
        ),
        in_specs=[hbm] * 3,
        out_specs=[hbm] * 3,
        scratch_shapes=[
            pltpu.VMEM((TILES, BAGS, DIM), bf16),
            pltpu.VMEM((ROWS, DIM), bf16),
            pltpu.VMEM((ROWS, DIM), f32),
            dma((10,)),
            dma((10,)),
        ],
        compiler_params=pltpu.CompilerParams(vmem_limit_bytes=60 << 20),
        name="hand_over",
    )(pooled, new_rows, new_state)
    return (pooled.reshape(TILES * BAGS, DIM), new_rows, new_state)


def solution(mesh):
    return jax.shard_map(
        per_device,
        mesh=mesh,
        in_specs=(
            P("table", "col"),
            P("table", "col"),
            P(("table", "col"), None, None),
            P(("table", "col"), None),
            P(("table", "col"), None),
            P(("table", "col"), None),
            P(("table", "col"), None),
        ),
        out_specs=(P(("table", "col"), None), P(("table", "col"), None), P(("table", "col"), None)),
        check_vma=False,
    )
```
